256 devices in a mesh: pop: 32 (over x, z_hi, core), mp: 8 (over y, z_lo).
Axes of the slice: x: 4, y: 4, z: 8 (z_hi: 4, z_lo: 2; z = z_hi * 2 + z_lo), core: 2. Of those that a mesh axis runs over, the one named last changes fastest.
Arguments:
- inputs: bfloat16 [64, 256, 4096], P('pop'), may hold values from -6 to 6
- mix_key: float32 [4096], replicated, may hold values from 0.05 to 0.95
- key_weight: bfloat16 [4096, 8192], P('pop', 'mp'), may hold values from -0.09375 to 0.09375
- value_weight: bfloat16 [8192, 4096], P('mp', 'pop'), may hold values from -0.0625 to 0.0625
- key_left: bfloat16 [64, 4096], P('pop'), may hold values from -6 to 6
- key_right: bfloat16 [64, 8192], P('pop', 'mp'), may hold values from -6 to 6
- value_left: bfloat16 [64, 8192], P('pop', 'mp'), may hold values from -6 to 6
- value_right: bfloat16 [64, 4096], P('pop'), may hold values from -6 to 6
- pair_sign: int32 [64], P('pop'), may hold values from -1 to 1, as said below
- targets: bfloat16 [64, 256, 4096], P('pop', None, 'mp')
Outputs:
- outputs: bfloat16 [128, 256, 4096], P('pop', None, 'mp')
- key_update: float32 [4096, 8192], P('pop', 'mp')
- value_update: float32 [8192, 4096], P('mp', 'pop')
The draws below stay inside these ranges and needn't reach their ends.
Inputs may be any that keep to these rules, and one draw needn't show every extreme that they name: `pair_sign`: every entry is -1 or 1.
All inputs are finite; a program needn't handle non-finite values.
Results may differ from the reference program's by a relative error of at most 0.018.
Values may be sent and summed in bfloat16 or wider, within the bound.
No kernel may reach another device: no remote copies, remote signals or barrier semaphores. Data moves between devices by JAX's collectives and lax.ppermute only.
A program may use at most 128 MiB of HBM per device.

```python
import math
import jax
import jax.numpy as jnp
from jax import lax

D = 4096
FF = 8192
SEQ = 256
PAIRS = 64
N_MP = 8


def draw_pair_sign(key, part):
    key = jax.random.fold_in(key, 11)
    return (jax.random.randint(key, (PAIRS,), 0, 2) * 2 - 1).astype(jnp.int32)


def draw_targets(key, part):
    key = jax.random.fold_in(key, 7)
    pair_pos = jnp.arange(PAIRS, dtype=jnp.float32) / max(PAIRS - 1, 1)
    feat_pos = jnp.arange(D, dtype=jnp.float32) / max(D - 1, 1)
    noise = jax.random.normal(key, (PAIRS, SEQ, D), jnp.float32)
    scale = (1.0 + 1.5 * pair_pos)[:, None, None] * (0.6 + 0.8 * feat_pos)[None, None, :]
    values = noise * scale
    return values.astype(jnp.bfloat16)


def shard_levels(rng, extent, shards, least, largest):
    gain, own = 1.0, jax.random.fold_in(rng, 6)
    for dim, shards_of in shards:
        heights = jnp.exp(jax.random.uniform(jax.random.fold_in(own, dim), (shards_of,), jnp.float32, least / len(shards), largest / len(shards)))
        gain = gain * jnp.repeat(heights, extent[dim] // shards_of).reshape([-1 if axis == dim else 1 for axis in range(len(extent))])
    return gain


def bell_draw(stream_key, extent, scale, limit, cuts=(), kind=jnp.bfloat16):
    drawn = jax.random.normal(stream_key, extent, jnp.float32) * scale
    if len(cuts) > 0:
        drawn = shard_levels(stream_key, extent, cuts, -0.22, 0.18) * drawn
    return jnp.clip(drawn, min=-limit, max=limit).astype(kind)


def setup_inputs(seed: int = 0) -> dict:
    seeds = jax.random.split(jax.random.key(seed), 11)
    return {
        "inputs": bell_draw(seeds[0], (PAIRS, SEQ, D), 1.0, 6.0, ((0, 32),)),
        "mix_key": jnp.clip(jax.random.uniform(seeds[1], (D,), jnp.float32, 0.05, 0.95), 0.05, 0.95),
        "key_weight": bell_draw(seeds[2], (D, FF), D ** -0.5, 0.09375, ((0, 32), (1, 8))),
        "value_weight": bell_draw(seeds[3], (FF, D), FF ** -0.5, 0.0625, ((0, 8), (1, 32))),
        "key_left": bell_draw(seeds[4], (PAIRS, D), 1.0, 6.0, ((0, 32),)),
        "key_right": bell_draw(seeds[5], (PAIRS, FF), 1.0, 6.0, ((0, 32), (1, 8))),
        "value_left": bell_draw(seeds[6], (PAIRS, FF), 1.0, 6.0, ((0, 32), (1, 8))),
        "value_right": bell_draw(seeds[7], (PAIRS, D), 1.0, 6.0, ((0, 32),)),
        "pair_sign": draw_pair_sign(jax.random.fold_in(seeds[10], 71), 0),
        "targets": draw_targets(jax.random.fold_in(seeds[10], 71), 0),
    }


def reference(inputs, mix_key, key_weight, value_weight, key_left, key_right, value_left, value_right, pair_sign, targets):
    block_width = FF // N_MP
    value_blocks = value_weight.reshape(N_MP, block_width, D)

    def one_pair(packed):
        pair_in, left_vec, right_vec, vleft_vec, vright_vec, sign_val, target_vals = packed
        current = pair_in.astype(jnp.float32)
        shifted = jnp.concatenate([jnp.zeros((1, D), jnp.float32), current[:-1]], 0)
        mixed_in = (current + (shifted - current) * mix_key).astype(jnp.bfloat16)
        base_act = jnp.dot(mixed_in, key_weight, preferred_element_type=jnp.float32)
        probe_dot = jnp.dot(mixed_in, left_vec, preferred_element_type=jnp.float32) / math.sqrt(D)
        sign_f = sign_val.astype(jnp.float32)
        member_sign = jnp.stack([sign_f, -sign_f])
        nudge_term = 0.5 * probe_dot[:, None] * right_vec.astype(jnp.float32)[None, :]
        pre_act = base_act[None] + member_sign[:, None, None] * nudge_term[None]
        hidden = (jnp.maximum(pre_act, 0.0) ** 2).astype(jnp.bfloat16).reshape(2 * SEQ, FF)
        row_sign = jnp.repeat(member_sign, SEQ)
        accum = jnp.zeros((2 * SEQ, D), jnp.float32)
        for block_index in range(N_MP):
            hidden_piece = hidden[:, block_index * block_width:(block_index + 1) * block_width]
            left_piece = vleft_vec[block_index * block_width:(block_index + 1) * block_width]
            side_coef = jnp.dot(hidden_piece, left_piece, preferred_element_type=jnp.float32) * (0.5 / math.sqrt(FF)) * row_sign
            block_term = jnp.dot(hidden_piece, value_blocks[block_index], preferred_element_type=jnp.float32)
            block_term = block_term + side_coef[:, None] * vright_vec.astype(jnp.float32)[None, :]
            rounded = lax.optimization_barrier(block_term.astype(jnp.bfloat16)).astype(jnp.float32)
            accum = accum + rounded
        out_vals = accum.astype(jnp.bfloat16).reshape(2, SEQ, D)
        gap_vals = out_vals.astype(jnp.float32) - target_vals.astype(jnp.float32)[None]
        return (out_vals, lax.optimization_barrier(jnp.mean(gap_vals * gap_vals, axis=(1, 2))))
    out_all, member_err = lax.map(one_pair, (inputs, key_left, key_right, value_left, value_right, pair_sign, targets))
    outputs = out_all.reshape(2 * PAIRS, SEQ, D)
    flat_err = member_err.reshape(-1)
    center_err = jnp.mean(flat_err)
    spread = jnp.sqrt(jnp.mean((flat_err - center_err) ** 2) + 1e-05)
    pair_coef = pair_sign.astype(jnp.float32) * (member_err[:, 0] - member_err[:, 1]) / (spread * math.sqrt(PAIRS))
    dims = (((0,), (0,)), ((), ()))
    key_update = lax.dot_general(key_left.astype(jnp.float32) * pair_coef[:, None], key_right.astype(jnp.float32), dims, precision=lax.Precision.HIGHEST)
    value_update = lax.dot_general(value_left.astype(jnp.float32) * pair_coef[:, None], value_right.astype(jnp.float32), dims, precision=lax.Precision.HIGHEST)
    return (outputs, key_update, value_update)
```

```python
import functools
import math

import jax
import jax.numpy as jnp
from jax import lax
from jax.experimental import pallas as pl
from jax.experimental.pallas import tpu as pltpu
from jax.sharding import PartitionSpec as P

FF = 8192
D = 4096
SEQ = 256
BF = jnp.bfloat16
F32 = jnp.float32
AXES = ("pop", "mp")
SIZES = dict(x=4, zh=4, c=2, y=4, zl=2)
RING = (0, -1, 1, 2)


def place(x, zh, c, y, zl):
    return ((x * 4 + zh) * 2 + c) * 8 + y * 2 + zl


def everywhere():
    for x in range(4):
        for zh in range(4):
            for c in range(2):
                for y in range(4):
                    for zl in range(2):
                        yield dict(x=x, zh=zh, c=c, y=y, zl=zl)


def move(value, **shift):
    pairs = []
    for at in everywhere():
        to = {k: (v + shift.get(k, 0)) % SIZES[k] for k, v in at.items()}
        pairs.append((place(**at), place(**to)))
    return lax.ppermute(value, AXES, pairs)


def transpose_xy(value):
    pairs = []
    for at in everywhere():
        pairs.append((place(**at), place(**{**at, "x": at["y"], "y": at["x"]})))
    return lax.ppermute(value, AXES, pairs)


def after(value, *others):
    return lax.optimization_barrier((value, *others))[0]


def params(mib):
    return pltpu.CompilerParams(vmem_limit_bytes=mib * 2**20)


def mix_kernel(x_ref, mix_ref, left_ref, out_ref, probe_ref):
    step = pl.program_id(1)
    cur = x_ref[0].astype(F32)
    row = lax.broadcasted_iota(jnp.int32, cur.shape, 0)
    shifted = jnp.where(row == 0, 0.0, pltpu.roll(cur, 1, 0))
    mixed = (cur + (shifted - cur) * mix_ref[...]).astype(BF)
    prod = mixed.astype(F32) * left_ref[0]
    part = prod[:, :128]
    for i in range(1, 8):
        part = part + prod[:, i * 128 : (i + 1) * 128]

    @pl.when(step == 0)
    def _():
        probe_ref[0] = part

    @pl.when(step != 0)
    def _():
        probe_ref[0] += part

    for zh in range(4):
        out_ref[zh] = mixed[:, zh * 256 : (zh + 1) * 256]


def mix(inputs, mix_key, key_left):
    return pl.pallas_call(
        mix_kernel,
        grid=(2, 4),
        in_specs=[
            pl.BlockSpec((1, SEQ, 1024), lambda p, x: (p, 0, x)),
            pl.BlockSpec((1, 1024), lambda p, x: (0, x)),
            pl.BlockSpec((1, 1, 1024), lambda p, x: (p, 0, x)),
        ],
        out_specs=[
            pl.BlockSpec((4, SEQ, 256), lambda p, x: (0, p, x)),
            pl.BlockSpec((1, SEQ, 128), lambda p, x: (p, 0, 0)),
        ],
        out_shape=[
            jax.ShapeDtypeStruct((4, 2 * SEQ, 1024), BF),
            jax.ShapeDtypeStruct((2, SEQ, 128), F32),
        ],
        compiler_params=params(16),
        cost_estimate=pl.CostEstimate(flops=8 * 2**20, bytes_accessed=8 * 2**20, transcendentals=0),
        name="mix",
    )(inputs, mix_key.reshape(1, D), key_left.astype(F32).reshape(2, 1, D))


def key_kernel(first, last, s_ref, a_ref, *refs):
    own, other = refs[:4], refs[4:8]
    refs = refs[8:]
    if not first:
        acc, refs = refs[:2], refs[2:]
    outs, w_ref = refs[:2], refs[2]
    x, c = s_ref[1], s_ref[2]
    mine = pl.multiple_of(c * 128, 128)
    its = pl.multiple_of((1 - c) * 128, 128)
    for k, rel in enumerate(RING):
        at = lax.rem(x + rel + 4, 4)
        w_ref[at, pl.ds(mine, 128), :] = own[k][...]
        w_ref[at, pl.ds(its, 128), :] = other[k][...]
    for p in range(2):
        total = jnp.dot(
            a_ref[0, p * SEQ : (p + 1) * SEQ, :],
            w_ref[...].reshape(1024, 1024),
            preferred_element_type=F32,
        )
        if not first:
            total = total + acc[p][...]
        outs[p][...] = total.astype(outs[p].dtype)


def key_step(scalars, mixed, own, other, acc, last):
    first = acc is None
    whole = lambda shape: pl.BlockSpec(shape, lambda i, s: (0,) * len(shape))
    args = [mixed, *own, *other] + ([] if first else list(acc))
    specs = [pl.BlockSpec((1, 2 * SEQ, 1024), lambda i, s: (s[0], 0, 0))]
    specs += [whole((128, 1024))] * 8 + ([] if first else [whole((SEQ, 1024))] * 2)
    out = jax.ShapeDtypeStruct((SEQ, 1024), BF if last else F32)
    return pl.pallas_call(
        functools.partial(key_kernel, first, last),
        grid_spec=pltpu.PrefetchScalarGridSpec(
            num_scalar_prefetch=1,
            grid=(1,),
            in_specs=specs,
            out_specs=[whole((SEQ, 1024))] * 2,
            scratch_shapes=[pltpu.VMEM((4, 256, 1024), BF)],
        ),
        out_shape=[out, out],
        compiler_params=params(24),
        cost_estimate=pl.CostEstimate(flops=2**30, bytes_accessed=2**20, transcendentals=0),
        name="key_step",
    )(scalars, *args)


def value_kernel(s_ref, *refs):
    base, refs = refs[:5], refs[5:]
    probe_ref, vec_ref, right_ref = refs[:3]
    own, other = refs[3:8], refs[8:13]
    send_ref, keep_ref, h_ref, w_ref, side_ref = refs[13:]
    j = pl.program_id(0)
    x, c, y, sign = s_ref[4], s_ref[5], s_ref[6], s_ref[7].astype(F32)

    @pl.when(j == 0)
    def _():
        for rows in range(2):
            lo, hi = rows * 128, (rows + 1) * 128
            probe = jnp.sum(probe_ref[0, lo:hi, :], axis=1, keepdims=True)
            probe = probe * (0.5 * sign / math.sqrt(D))
            side = [jnp.zeros((128, 128), F32), jnp.zeros((128, 128), F32)]
            for k, rel in enumerate(RING):
                at = lax.rem(y + rel + 4, 4)
                for piece in range(4):
                    cols = slice(piece * 256, (piece + 1) * 256)
                    if k < 3:
                        act = base[k][lo:hi, cols].astype(F32)
                    else:
                        act = base[3 + rows][:, cols].astype(F32)
                    nudge = probe * vec_ref[k, 0:1, cols]
                    left = vec_ref[k, 1:2, cols]
                    for m, pre in enumerate((act + nudge, act - nudge)):
                        pre = jnp.maximum(pre, 0.0)
                        hid = (pre * pre).astype(BF)
                        h_ref[at, m * SEQ + lo : m * SEQ + hi, cols] = hid
                        prod = hid.astype(F32) * left
                        side[m] = side[m] + prod[:, :128] + prod[:, 128:]
            scale = 0.5 / math.sqrt(FF) * sign
            for m in range(2):
                total = jnp.sum(side[m], axis=1, keepdims=True) * (scale if m == 0 else -scale)
                side_ref[m * SEQ + lo : m * SEQ + hi, :] = jnp.broadcast_to(total, (128, 128))

    def pair(k, lo, hi):
        mine, its = own[k][0], other[k][0]
        at = lax.rem(x + RING[min(k, 3)] + 4, 4)
        w_ref[at, lo:hi, 0:128] = jnp.where(c == 0, mine, its)
        w_ref[at, lo:hi, 128:256] = jnp.where(c == 0, its, mine)

    for k in range(3):
        pair(k, 0, 1024)
    pair(3, 0, 512)
    pair(4, 512, 1024)

    for m in range(2):
        rows = slice(m * SEQ, (m + 1) * SEQ)
        total = jnp.dot(h_ref[0, rows, :], w_ref[0], preferred_element_type=F32)
        for a in range(1, 4):
            total = total + jnp.dot(h_ref[a, rows, :], w_ref[a], preferred_element_type=F32)
        side = side_ref[rows, :]
        total = total + jnp.concatenate([side, side], axis=1) * right_ref[0]

        @pl.when(j < 2)
        def _():
            send_ref[rows, :] = total.astype(BF)

        @pl.when(j >= 2)
        def _():
            keep_ref[rows, :] = total


def value_step(scalars, base, probe, vecs, right, own, other, pair):
    whole = lambda shape: pl.BlockSpec(shape, lambda j, s: (0,) * len(shape))
    slot = lambda rows: pl.BlockSpec((1, rows, 128), lambda j, s: (s[j], 0, 0))
    weights = [slot(1024)] * 3 + [slot(512)] * 2
    return pl.pallas_call(
        value_kernel,
        grid_spec=pltpu.PrefetchScalarGridSpec(
            num_scalar_prefetch=1,
            grid=(4,),
            in_specs=[whole((SEQ, 1024))] * 3
            + [whole((SEQ // 2, 1024))] * 2
            + [
                pl.BlockSpec((1, SEQ, 128), lambda j, s: (pair, 0, 0)),
                whole((4, 2, 1024)),
                pl.BlockSpec((1, 1, 256), lambda j, s: (s[8 + j], 0, 0)),
            ]
            + weights * 2,
            out_specs=[
                pl.BlockSpec((2 * SEQ, 256), lambda j, s: (0, jnp.minimum(j, 1))),
                pl.BlockSpec((2 * SEQ, 256), lambda j, s: (0, jnp.maximum(j - 2, 0))),
            ],
            scratch_shapes=[
                pltpu.VMEM((4, 2 * SEQ, 1024), BF),
                pltpu.VMEM((4, 1024, 256), BF),
                pltpu.VMEM((2 * SEQ, 128), F32),
            ],
        ),
        out_shape=[
            jax.ShapeDtypeStruct((2 * SEQ, 512), BF),
            jax.ShapeDtypeStruct((2 * SEQ, 512), F32),
        ],
        compiler_params=params(32),
        cost_estimate=pl.CostEstimate(flops=5 * 2**30, bytes_accessed=2**22, transcendentals=0),
        name="value_step",
    )(scalars, *base, probe, vecs, right, *own, *other)


def finish_kernel(keep0, got0, keep1, got1, target_ref, out_ref, err_ref):
    p = pl.program_id(0)
    target = target_ref[0].astype(F32)
    lane = lax.broadcasted_iota(jnp.int32, (1, 128), 1)

    @pl.when(p == 0)
    def _():
        err_ref[...] = jnp.zeros_like(err_ref)

    for pair, keep, got in ((0, keep0, got0), (1, keep1, got1)):

        @pl.when(p == pair)
        def _(pair=pair, keep=keep, got=got):
            for m in range(2):
                rows = slice(m * SEQ, (m + 1) * SEQ)
                out = (keep[rows, :] + got[rows, :].astype(F32)).astype(BF)
                out_ref[m] = out
                gap = out.astype(F32) - target
                err = jnp.sum(gap * gap)
                err_ref[...] += jnp.where(lane == 2 * pair + m, err, 0.0)


def finish(keep, got, targets):
    whole = pl.BlockSpec((2 * SEQ, 512), lambda p: (0, 0))
    return pl.pallas_call(
        finish_kernel,
        grid=(2,),
        in_specs=[whole] * 4 + [pl.BlockSpec((1, SEQ, 512), lambda p: (p, 0, 0))],
        out_specs=[
            pl.BlockSpec((2, SEQ, 512), lambda p: (p, 0, 0)),
            pl.BlockSpec((1, 128), lambda p: (0, 0)),
        ],
        out_shape=[
            jax.ShapeDtypeStruct((4, SEQ, 512), BF),
            jax.ShapeDtypeStruct((1, 128), F32),
        ],
        compiler_params=params(24),
        cost_estimate=pl.CostEstimate(flops=2**21, bytes_accessed=2**22, transcendentals=0),
        name="finish",
    )(keep[0], got[0], keep[1], got[1], targets)


def ring4(value, axis):
    below, above = move(value, **{axis: 1}), move(value, **{axis: -1})
    return [value, below, above, move(below, **{axis: 1})]


def sum4(value, axis):
    got = [move(value, **{axis: s}) for s in (1, -1, 2)]
    return (value + got[0]) + (got[1] + got[2])


def outer(left, right):
    high = left.astype(BF)
    low = (left - high.astype(F32)).astype(BF)
    left = jnp.concatenate([high, low], 0)
    right = jnp.concatenate([right, right], 0)
    return lax.dot_general(left, right, (((0,), (0,)), ((), ())), preferred_element_type=F32)


def per_device(
    inputs,
    mix_key,
    key_weight,
    value_weight,
    key_left,
    key_right,
    value_left,
    value_right,
    pair_sign,
    targets,
):
    pop, mp = lax.axis_index("pop"), lax.axis_index("mp")
    x, zh, c = pop // 8, (pop // 2) % 4, pop % 2
    y, zl = mp // 2, mp % 2
    i32 = lambda *v: jnp.stack([jnp.asarray(e, jnp.int32) for e in v])

    key_z = ring4(key_weight, "zh")
    mixed, probe = mix(inputs, mix_key, key_left)
    acc = None
    for k, rel in enumerate(RING):
        piece = key_z[k]
        below, above = move(piece, x=1), move(piece, x=-1)
        far = move(below, x=1) if k % 2 == 0 else move(above, x=-1)
        own = [piece, below, above, far]
        other = [move(v, c=1) for v in own]
        acc = key_step(i32((zh + rel) % 4, x, c), mixed, own, other, acc, k == 3)
    base = acc

    moved = transpose_xy(value_weight)
    value_z = jnp.stack(ring4(moved, "zh"))
    below, above = move(value_z, x=1), move(value_z, x=-1)
    far0, far1 = move(below[:, :512], x=1), move(above[:, 512:], x=-1)
    own_v = [value_z, below, above, far0, far1]
    other_v = [move(v, c=1) for v in own_v]

    vec = jnp.concatenate([key_right, value_left], 0)
    vecs = jnp.stack(ring4(vec, "y")).astype(F32)
    right = lax.dynamic_slice_in_dim(value_right.astype(F32), y * 1024, 1024, 1)

    def to_owner(v):
        return v.reshape(2, 32, 128).transpose(1, 0, 2)

    def to_all(v):
        return jnp.broadcast_to(v.reshape(1, 16, 128), (32, 16, 128))

    sign = pair_sign.astype(BF)[:, None]
    parcel = jnp.concatenate(
        [
            to_owner(key_left * sign),
            to_owner(value_right),
            to_all(key_right),
            to_all(value_left * sign),
        ],
        1,
    )
    parcel = lax.all_to_all(parcel, "pop", split_axis=0, concat_axis=0, tiled=True)
    left_key = parcel[:, 0:2].reshape(64, 128).astype(F32)
    right_value = parcel[:, 2:4].reshape(64, 128)
    right_key = parcel[:, 4:20].reshape(64, 1024)
    left_value = parcel[:, 20:36].reshape(64, 1024).astype(F32)

    column = [2 - 2 * zl, 3 - 2 * zl, 2 * zl, 2 * zl + 1]
    slots = []
    for col in column:
        rel = (col - zh) % 4
        slots.append(jnp.where(rel == 3, 1, jnp.where(rel == 0, 0, rel + 1)))
    keep, got = [], []
    for p in range(2):
        below, above = move(base[p], y=1), move(base[p], y=-1)
        blocks = [
            base[p],
            below,
            above,
            move(below[:128], y=1),
            move(above[128:], y=-1),
        ]
        scalars = i32(*slots, x, c, y, pair_sign[p], *column)
        send, kept = value_step(
            scalars,
            blocks,
            probe,
            vecs[:, p::2],
            right[p].reshape(4, 1, 256),
            own_v,
            other_v,
            p,
        )
        keep.append(kept)
        got.append(move(send, zl=1))
    outputs, err = finish(keep, got, targets)

    lane = lax.broadcasted_iota(jnp.int32, (1, 128), 1)
    err = jnp.tile(err[:, :4], (1, 32))
    err = jnp.where(lane // 4 == pop, err, 0.0)
    err = sum4(err, "y")
    err = err + move(err, zl=1)
    err = err + move(err, c=1)
    err = sum4(err, "x")
    err = sum4(err, "zh")
    member_err = err.reshape(128) / (SEQ * D)
    spread = jnp.sqrt(jnp.mean((member_err - jnp.mean(member_err)) ** 2) + 1e-05)
    both = member_err.reshape(64, 2)
    coef = ((both[:, 0] - both[:, 1]) / (spread * math.sqrt(64)))[:, None]
    key_update = outer(left_key * coef, right_key)
    value_update = outer(left_value * coef, right_value)
    return outputs, key_update, value_update


def solution(mesh):
    in_specs = (
        P("pop", None, None),
        P(),
        P("pop", "mp"),
        P("mp", "pop"),
        P("pop", None),
        P("pop", "mp"),
        P("pop", "mp"),
        P("pop", None),
        P("pop"),
        P("pop", None, "mp"),
    )
    out_specs = (P("pop", None, "mp"), P("pop", "mp"), P("mp", "pop"))
    return jax.shard_map(
        per_device, mesh=mesh, in_specs=in_specs, out_specs=out_specs, check_vma=False
    )
```

```python
import functools
import math

import jax
import jax.numpy as jnp
from jax import lax
from jax.experimental import pallas as pl
from jax.experimental.pallas import tpu as pltpu
from jax.sharding import PartitionSpec as P

FF = 8192
D = 4096
SEQ = 256
BF = jnp.bfloat16
F32 = jnp.float32
AXES = ("pop", "mp")
SIZES = dict(x=4, zh=4, c=2, y=4, zl=2)


def place(x, zh, c, y, zl):
    return ((x * 4 + zh) * 2 + c) * 8 + y * 2 + zl


def everywhere():
    for x in range(4):
        for zh in range(4):
            for c in range(2):
                for y in range(4):
                    for zl in range(2):
                        yield dict(x=x, zh=zh, c=c, y=y, zl=zl)


def move(value, **shift):
    pairs = []
    for at in everywhere():
        to = {k: (v + shift.get(k, 0)) % SIZES[k] for k, v in at.items()}
        pairs.append((place(**at), place(**to)))
    return lax.ppermute(value, AXES, pairs)


def step(value, axis):
    pairs = []
    for at in everywhere():
        to = {**at, axis: (at[axis] + (1 - 2 * at["c"])) % SIZES[axis]}
        pairs.append((place(**at), place(**to)))
    return lax.ppermute(value, AXES, pairs)


def ring(value, axis):
    out = [value]
    for _ in range(SIZES[axis] - 1):
        out.append(step(out[-1], axis))
    return out


def transpose_xy(value):
    pairs = []
    for at in everywhere():
        pairs.append((place(**at), place(**{**at, "x": at["y"], "y": at["x"]})))
    return lax.ppermute(value, AXES, pairs)


def params(mib):
    return pltpu.CompilerParams(vmem_limit_bytes=mib * 2**20)


def mix_kernel(x_ref, mix_ref, left_ref, out_ref, probe_ref):
    step = pl.program_id(1)
    cur = x_ref[0].astype(F32)
    row = lax.broadcasted_iota(jnp.int32, cur.shape, 0)
    shifted = jnp.where(row == 0, 0.0, pltpu.roll(cur, 1, 0))
    mixed = (cur + (shifted - cur) * mix_ref[...]).astype(BF)
    prod = mixed.astype(F32) * left_ref[0]
    part = prod[:, :128]
    for i in range(1, 8):
        part = part + prod[:, i * 128 : (i + 1) * 128]

    @pl.when(step == 0)
    def _():
        probe_ref[0] = part

    @pl.when(step != 0)
    def _():
        probe_ref[0] += part

    for zh in range(4):
        for c in range(2):
            col = zh * 256 + c * 128
            out_ref[zh, c] = mixed[:, col : col + 128]


def mix(inputs, mix_key, key_left):
    return pl.pallas_call(
        mix_kernel,
        grid=(2, 4),
        in_specs=[
            pl.BlockSpec((1, SEQ, 1024), lambda p, x: (p, 0, x)),
            pl.BlockSpec((1, 1024), lambda p, x: (0, x)),
            pl.BlockSpec((1, 1, 1024), lambda p, x: (p, 0, x)),
        ],
        out_specs=[
            pl.BlockSpec((4, 2, SEQ, 128), lambda p, x: (0, 0, p, x)),
            pl.BlockSpec((1, SEQ, 128), lambda p, x: (p, 0, 0)),
        ],
        out_shape=[
            jax.ShapeDtypeStruct((4, 2, 2 * SEQ, 512), BF),
            jax.ShapeDtypeStruct((2, SEQ, 128), F32),
        ],
        compiler_params=params(16),
        cost_estimate=pl.CostEstimate(flops=8 * 2**20, bytes_accessed=8 * 2**20, transcendentals=0),
        name="mix",
    )(inputs, mix_key.reshape(1, D), key_left.astype(F32).reshape(2, 1, D))


def join_kernel(a_ref, b_ref, _, out_ref):
    out_ref[:128] = a_ref[...]
    out_ref[128:] = b_ref[...]


def join(pair, token):
    whole = pl.BlockSpec((128, 1024), lambda: (0, 0))
    return pl.pallas_call(
        join_kernel,
        in_specs=[whole, whole, pl.BlockSpec(memory_space=pl.ANY)],
        out_specs=pl.BlockSpec((256, 1024), lambda: (0, 0)),
        out_shape=jax.ShapeDtypeStruct((256, 1024), BF),
        compiler_params=params(4),
        cost_estimate=pl.CostEstimate(flops=0, bytes_accessed=2**20, transcendentals=0),
        name="join",
    )(*pair, token)


def key_kernel(layout, count, first, s_ref, a_ref, *refs):
    pieces, refs = refs[:count], refs[count:]
    if not first:
        acc, refs = refs[:2], refs[2:]
    outs, w_ref = refs[:2], refs[2]
    x, zh, c = s_ref[0], s_ref[1], s_ref[2]
    way = 2 * c - 1
    total = None if first else jnp.concatenate([acc[0][...], acc[1][...]], 0)
    for g, (back, places) in enumerate(layout):
        for half in range(2):
            core = c if half == 0 else 1 - c
            sign = way if half == 0 else -way
            for i in range(4):
                n, row = places[half * 4 + i]
                at = lax.rem(x + sign * i + 4, 4)
                w_ref[g, half, at] = pieces[n][row : row + 128, :]
            part = jnp.dot(
                a_ref[lax.rem(zh + sign * back + 4, 4), core],
                w_ref[g, half].reshape(512, 1024),
                preferred_element_type=F32,
            )
            total = part if total is None else total + part
    for p in range(2):
        outs[p][...] = total[p * SEQ : (p + 1) * SEQ].astype(outs[p].dtype)


def key_step(scalars, mixed, pieces, layout, acc, last):
    first = acc is None
    whole = lambda shape: pl.BlockSpec(shape, lambda i, s: (0,) * len(shape))
    args = [mixed, *pieces] + ([] if first else list(acc))
    specs = [whole((4, 2, 2 * SEQ, 512))]
    specs += [whole(v.shape) for v in pieces] + ([] if first else [whole((SEQ, 1024))] * 2)
    out = jax.ShapeDtypeStruct((SEQ, 1024), BF if last else F32)
    return pl.pallas_call(
        functools.partial(key_kernel, layout, len(pieces), first),
        grid_spec=pltpu.PrefetchScalarGridSpec(
            num_scalar_prefetch=1,
            grid=(1,),
            in_specs=specs,
            out_specs=[whole((SEQ, 1024))] * 2,
            scratch_shapes=[pltpu.VMEM((len(layout), 2, 4, 128, 1024), BF)],
        ),
        out_shape=[out, out],
        compiler_params=params(40),
        cost_estimate=pl.CostEstimate(
            flops=len(layout) * 2**30, bytes_accessed=2**20, transcendentals=0
        ),
        name="key_step",
    )(scalars, *args)


def order_kernel(s_ref, *refs):
    for k in range(4):
        for half in range(2):

            @pl.when(s_ref[k] // 2 == half)
            def _(k=k, half=half):
                refs[4 + half][lax.rem(s_ref[k], 2)] = refs[k][...]


def order(scalars, pieces):
    whole = lambda shape: pl.BlockSpec(shape, lambda i, s: (0,) * len(shape))
    return pl.pallas_call(
        order_kernel,
        grid_spec=pltpu.PrefetchScalarGridSpec(
            num_scalar_prefetch=1,
            grid=(1,),
            in_specs=[whole((1024, 128))] * 4,
            out_specs=[whole((2, 1024, 128))] * 2,
        ),
        out_shape=[jax.ShapeDtypeStruct((2, 1024, 128), BF)] * 2,
        compiler_params=params(8),
        cost_estimate=pl.CostEstimate(flops=0, bytes_accessed=2**21, transcendentals=0),
        name="order",
    )(scalars, *pieces)


def hidden_kernel(s_ref, b0, b1, b2, b3, probe_ref, vec_ref, h_ref, side_ref):
    base = (b0, b1, b2, b3)
    y, way, sign = s_ref[0], 2 * s_ref[1] - 1, s_ref[2].astype(F32)
    probe_all = jnp.sum(probe_ref[0], axis=1, keepdims=True) * (0.5 * sign / math.sqrt(D))
    side_ref[...] = jnp.zeros_like(side_ref)
    for k in range(4):
        at = lax.rem(y + way * k + 4, 4)
        for lo in range(0, SEQ, 128):
            rows = slice(lo, lo + 128)
            side = [jnp.zeros((128, 128), F32), jnp.zeros((128, 128), F32)]
            for col in range(0, 1024, 256):
                cols = slice(col, col + 256)
                to = pl.ds(pl.multiple_of(at * 1024 + col, 256), 256)
                act = base[k][rows, cols].astype(F32)
                nudge = probe_all[rows] * vec_ref[at, 0:1, cols]
                left = vec_ref[at, 1:2, cols]
                for m, pre in enumerate((act + nudge, act - nudge)):
                    pre = jnp.maximum(pre, 0.0)
                    hid = (pre * pre).astype(BF)
                    h_ref[m * SEQ + lo : m * SEQ + lo + 128, to] = hid
                    prod = hid.astype(F32) * left
                    side[m] = side[m] + prod[:, :128] + prod[:, 128:]
            for m in range(2):
                side_ref[m * SEQ + lo : m * SEQ + lo + 128, :] += side[m]
    scale = 0.5 / math.sqrt(FF) * sign
    for m in range(2):
        rows = slice(m * SEQ, (m + 1) * SEQ)
        total = jnp.sum(side_ref[rows, :], axis=1, keepdims=True) * (scale if m == 0 else -scale)
        side_ref[rows, :] = jnp.broadcast_to(total, (SEQ, 128))


def hidden_step(scalars, base, probe, vecs, pair):
    whole = lambda shape: pl.BlockSpec(shape, lambda i, s: (0,) * len(shape))
    return pl.pallas_call(
        hidden_kernel,
        grid_spec=pltpu.PrefetchScalarGridSpec(
            num_scalar_prefetch=1,
            grid=(1,),
            in_specs=[whole((SEQ, 1024))] * 4
            + [pl.BlockSpec((1, SEQ, 128), lambda i, s: (pair, 0, 0)), whole((4, 2, 1024))],
            out_specs=[whole((2 * SEQ, 4096)), whole((2 * SEQ, 128))],
        ),
        out_shape=[
            jax.ShapeDtypeStruct((2 * SEQ, 4096), BF),
            jax.ShapeDtypeStruct((2 * SEQ, 128), F32),
        ],
        compiler_params=params(20),
        cost_estimate=pl.CostEstimate(flops=2**25, bytes_accessed=2**22, transcendentals=0),
        name="hidden",
    )(scalars, *base, probe, vecs)


def value_kernel(s_ref, h_ref, side_ref, right_ref, *refs):
    own, other, out_ref, w_ref = refs[:4], refs[4:8], refs[8], refs[9]
    x, c = s_ref[0], s_ref[1]
    for k in range(4):
        for core, blocks in ((c, own), (1 - c, other)):
            at = pl.multiple_of(lax.rem(x + (2 * core - 1) * k + 4, 4) * 1024, 1024)
            for n in range(2):
                col = pl.multiple_of(core * 128 + n * 256, 128)
                w_ref[pl.ds(at, 1024), pl.ds(col, 128)] = blocks[k][n]
    total = jnp.dot(h_ref[...], w_ref[...], preferred_element_type=F32)
    for n in range(4):
        cols = slice(n * 128, (n + 1) * 128)
        out = total[:, cols] + side_ref[...] * right_ref[:, cols]
        out_ref[:, cols] = out.astype(out_ref.dtype)


def value_step(scalars, hidden, side, right, own, other, dtype):
    whole = lambda shape: pl.BlockSpec(shape, lambda i, s: (0,) * len(shape))
    return pl.pallas_call(
        value_kernel,
        grid_spec=pltpu.PrefetchScalarGridSpec(
            num_scalar_prefetch=1,
            grid=(1,),
            in_specs=[whole((2 * SEQ, 4096)), whole((2 * SEQ, 128)), whole((1, 512))]
            + [whole((2, 1024, 128))] * 8,
            out_specs=whole((2 * SEQ, 512)),
            scratch_shapes=[pltpu.VMEM((4096, 512), BF)],
        ),
        out_shape=jax.ShapeDtypeStruct((2 * SEQ, 512), dtype),
        compiler_params=params(32),
        cost_estimate=pl.CostEstimate(flops=2**31, bytes_accessed=2**23, transcendentals=0),
        name="value",
    )(scalars, hidden, side, right, *own, *other)


def finish_kernel(keep0, got0, keep1, got1, target_ref, out_ref, err_ref):
    p = pl.program_id(0)
    target = target_ref[0].astype(F32)
    lane = lax.broadcasted_iota(jnp.int32, (1, 128), 1)

    @pl.when(p == 0)
    def _():
        err_ref[...] = jnp.zeros_like(err_ref)

    for pair, keep, got in ((0, keep0, got0), (1, keep1, got1)):

        @pl.when(p == pair)
        def _(pair=pair, keep=keep, got=got):
            for m in range(2):
                rows = slice(m * SEQ, (m + 1) * SEQ)
                out = (keep[rows, :] + got[rows, :].astype(F32)).astype(BF)
                out_ref[m] = out
                gap = out.astype(F32) - target
                err = jnp.sum(gap * gap)
                err_ref[...] += jnp.where(lane == 2 * pair + m, err, 0.0)


def finish(keep, got, targets):
    whole = pl.BlockSpec((2 * SEQ, 512), lambda p: (0, 0))
    return pl.pallas_call(
        finish_kernel,
        grid=(2,),
        in_specs=[whole] * 4 + [pl.BlockSpec((1, SEQ, 512), lambda p: (p, 0, 0))],
        out_specs=[
            pl.BlockSpec((2, SEQ, 512), lambda p: (p, 0, 0)),
            pl.BlockSpec((1, 128), lambda p: (0, 0)),
        ],
        out_shape=[
            jax.ShapeDtypeStruct((4, SEQ, 512), BF),
            jax.ShapeDtypeStruct((1, 128), F32),
        ],
        compiler_params=params(24),
        cost_estimate=pl.CostEstimate(flops=2**21, bytes_accessed=2**22, transcendentals=0),
        name="finish",
    )(keep[0], got[0], keep[1], got[1], targets)


def outer(left, right):
    high = left.astype(BF)
    low = (left - high.astype(F32)).astype(BF)
    left = jnp.concatenate([high, low], 0)
    right = jnp.concatenate([right, right], 0)
    return lax.dot_general(left, right, (((0,), (0,)), ((), ())), preferred_element_type=F32)


def update_kernel(err_ref, lk_ref, rk_ref, lv_ref, rv_ref, key_ref, value_ref):
    err = jnp.sum(err_ref[...], axis=1) / (SEQ * D)
    lane = lax.broadcasted_iota(jnp.int32, err.shape, 1)
    used = lane < 4
    mean = jnp.sum(jnp.where(used, err, 0.0)) / 128
    var = jnp.sum(jnp.where(used, (err - mean) * (err - mean), 0.0)) / 128
    spread = jnp.sqrt(jnp.full((1, 1), var + 1e-05, F32))
    diff = err - pltpu.roll(err, 127, 1)
    coef = jnp.concatenate([diff[:, 0:1], diff[:, 2:3]], 0) / (spread * math.sqrt(64))
    key_ref[...] = outer(lk_ref[...].astype(F32) * coef, rk_ref[...])
    value_ref[...] = outer(lv_ref[...].astype(F32) * coef, rv_ref[...])


def update(err, left_key, right_key, left_value, right_value):
    return pl.pallas_call(
        update_kernel,
        out_shape=[
            jax.ShapeDtypeStruct((128, 1024), F32),
            jax.ShapeDtypeStruct((1024, 128), F32),
        ],
        compiler_params=params(8),
        cost_estimate=pl.CostEstimate(flops=2**26, bytes_accessed=2**21, transcendentals=0),
        name="update",
    )(err, left_key, right_key, left_value, right_value)


def per_device(
    inputs,
    mix_key,
    key_weight,
    value_weight,
    key_left,
    key_right,
    value_left,
    value_right,
    pair_sign,
    targets,
):
    pop, mp = lax.axis_index("pop"), lax.axis_index("mp")
    x, zh, c = pop // 8, (pop // 2) % 4, pop % 2
    y, zl = mp // 2, mp % 2
    i32 = lambda *v: jnp.stack([jnp.asarray(e, jnp.int32) for e in v])

    def swap(values):
        return [move(v, c=1) for v in values]

    key_x = [ring(key_weight, "x")]
    key_z = ring(key_weight, "zh")
    moved = transpose_xy(value_weight)
    mixed, probe = mix(inputs, mix_key, key_left)
    key_x.append(ring(join(key_z[1:3], probe), "x"))
    key_x.append(ring(key_z[3], "x"))
    me = i32(x, zh, c)
    plain = [(n, 0) for n in range(8)]
    wide = lambda row: [(n, row) for n in range(8)]
    acc = key_step(me, mixed, key_x[0] + swap(key_x[0]), [(0, plain)], None, False)
    acc = key_step(
        me, mixed, key_x[1] + swap(key_x[1]), [(1, wide(0)), (2, wide(128))], acc, False
    )
    base = key_step(me, mixed, key_x[2] + swap(key_x[2]), [(3, plain)], acc, True)

    slots = [(zh + (2 * c - 1) * k) % 4 for k in range(4)]
    slots = i32(*[jnp.where(s // 2 == zl, 2, 0) + s % 2 for s in slots])
    send_w, keep_w = order(slots, ring(moved, "zh"))
    send_w, keep_w = ring(send_w, "x"), ring(keep_w, "x")
    send_w, keep_w = (send_w, swap(send_w)), (keep_w, swap(keep_w))

    vec = jnp.concatenate([key_right, value_left], 0)
    vec = jnp.broadcast_to(vec[None], (4, 4, 1024))
    vec = lax.all_to_all(
        vec,
        "mp",
        split_axis=0,
        concat_axis=0,
        tiled=True,
        axis_index_groups=[[0, 2, 4, 6], [1, 3, 5, 7]],
    ).astype(F32)

    def to_owner(v):
        return v.reshape(2, 32, 128).transpose(1, 0, 2)

    def to_all(v):
        return jnp.broadcast_to(v.reshape(1, 16, 128), (32, 16, 128))

    sign = pair_sign.astype(BF)[:, None]
    parcel = jnp.concatenate(
        [
            to_owner(key_left * sign),
            to_owner(value_right),
            to_all(key_right),
            to_all(value_left * sign),
        ],
        1,
    )
    parcel = lax.all_to_all(parcel, "pop", split_axis=0, concat_axis=0, tiled=True)

    def unpack(lo, hi):
        v = parcel[:, lo:hi].reshape(32, 2, (hi - lo) // 2 * 128)
        return v.transpose(1, 0, 2).reshape(64, (hi - lo) // 2 * 128)

    left_key, right_value = unpack(0, 2), unpack(2, 4)
    right_key, left_value = unpack(4, 20), unpack(20, 36)

    near = [ring(b, "y") for b in base]
    right = value_right.astype(F32)
    send_right, keep_right = (
        lax.dynamic_slice_in_dim(right, (2 * y + half) * 512, 512, 1) for half in (1 - zl, zl)
    )
    hidden, got, keep = [], [], []
    for p in range(2):
        hid, side = hidden_step(i32(y, c, pair_sign[p]), near[p], probe, vec[:, p::2], p)
        hidden.append((hid, side))
        send = value_step(i32(x, c), hid, side, send_right[p : p + 1], *send_w, BF)
        got.append(move(send, zl=1))
    for p in range(2):
        keep.append(value_step(i32(x, c), *hidden[p], keep_right[p : p + 1], *keep_w, F32))
    outputs, err = finish(keep, got, targets)

    err = jnp.broadcast_to(err[None], (256, 1, 128))
    err = lax.all_to_all(err, AXES, split_axis=0, concat_axis=0, tiled=True)
    key_update, value_update = update(
        err.reshape(32, 8, 128), left_key, right_key, left_value, right_value
    )
    return outputs, key_update, value_update


def solution(mesh):
    in_specs = (
        P("pop", None, None),
        P(),
        P("pop", "mp"),
        P("mp", "pop"),
        P("pop", None),
        P("pop", "mp"),
        P("pop", "mp"),
        P("pop", None),
        P("pop"),
        P("pop", None, "mp"),
    )
    out_specs = (P("pop", None, "mp"), P("pop", "mp"), P("mp", "pop"))
    return jax.shard_map(
        per_device, mesh=mesh, in_specs=in_specs, out_specs=out_specs, check_vma=False
    )
```

```python
import functools
import math

import jax
import jax.numpy as jnp
from jax import lax
from jax.experimental import pallas as pl
from jax.experimental.pallas import tpu as pltpu
from jax.sharding import PartitionSpec as P

FF = 8192
D = 4096
SEQ = 256
BF = jnp.bfloat16
F32 = jnp.float32
AXES = ("pop", "mp")
SIZES = dict(x=4, zh=4, c=2, y=4, zl=2)


def place(x, zh, c, y, zl):
    return ((x * 4 + zh) * 2 + c) * 8 + y * 2 + zl


def everywhere():
    for x in range(4):
        for zh in range(4):
            for c in range(2):
                for y in range(4):
                    for zl in range(2):
                        yield dict(x=x, zh=zh, c=c, y=y, zl=zl)


def move(value, **shift):
    pairs = []
    for at in everywhere():
        to = {k: (v + shift.get(k, 0)) % SIZES[k] for k, v in at.items()}
        pairs.append((place(**at), place(**to)))
    return lax.ppermute(value, AXES, pairs)


def step(value, axis, way=1):
    pairs = []
    for at in everywhere():
        to = {**at, axis: (at[axis] + way * (1 - 2 * at["c"])) % SIZES[axis]}
        pairs.append((place(**at), place(**to)))
    return lax.ppermute(value, AXES, pairs)


def transpose_xy(value):
    pairs = []
    for at in everywhere():
        pairs.append((place(**at), place(**{**at, "x": at["y"], "y": at["x"]})))
    return lax.ppermute(value, AXES, pairs)


ANY = pl.BlockSpec(memory_space=pl.ANY)


def whole(shape):
    return pl.BlockSpec(shape, lambda *_: (0,) * len(shape))


def call(kernel, name, args, specs, outs, out_specs, *, grid=(1,), scalars=None, tokens=(), scratch=(), us=1):
    lead = 0 if scalars is None else 1

    def body(*refs):
        kernel(*refs[:lead], *refs[lead + len(tokens) :])

    return pl.pallas_call(
        body,
        grid_spec=pltpu.PrefetchScalarGridSpec(
            num_scalar_prefetch=lead,
            grid=grid,
            in_specs=[ANY] * len(tokens) + list(specs),
            out_specs=out_specs,
            scratch_shapes=list(scratch),
        ),
        out_shape=outs,
        compiler_params=pltpu.CompilerParams(vmem_limit_bytes=56 * 2**20),
        cost_estimate=pl.CostEstimate(flops=us * 2**30, bytes_accessed=2**20, transcendentals=0),
        name=name,
    )(*([scalars] if lead else []), *tokens, *args)


def array(shape, dtype):
    return jax.ShapeDtypeStruct(shape, dtype)


def fence(values, tokens=()):
    count = len(values)
    return pl.pallas_call(
        lambda *refs: None,
        in_specs=[ANY] * (count + len(tokens)),
        out_specs=[ANY] * count,
        out_shape=[array(v.shape, v.dtype) for v in values],
        input_output_aliases={i: i for i in range(count)},
        compiler_params=pltpu.CompilerParams(vmem_limit_bytes=56 * 2**20),
        name="fence",
    )(*values, *tokens)


def mix_kernel(
    s_ref, x_ref, mix_ref, left_ref, mine_ref, its_ref, probe_ref, in_buf, out_buf, in_sems, out_sems
):
    def load(i):
        p, x = lax.div(i, 4), lax.rem(i, 4)
        return pltpu.make_async_copy(
            x_ref.at[p, :, pl.ds(pl.multiple_of(x * 1024, 1024), 1024)], in_buf.at[i], in_sems.at[i]
        )

    def save(i):
        p, x = lax.div(i, 4), lax.rem(i, 4)
        rows = pl.ds(pl.multiple_of(p * SEQ, SEQ), SEQ)
        return [
            pltpu.make_async_copy(
                out_buf.at[i, :, core], ref.at[:, x, rows], out_sems.at[i, half]
            )
            for half, (core, ref) in enumerate(((s_ref[0], mine_ref), (1 - s_ref[0], its_ref)))
        ]

    for i in range(8):
        load(i).start()
    probe_ref[...] = jnp.zeros_like(probe_ref)
    row = lax.broadcasted_iota(jnp.int32, (SEQ, 256), 0)

    def one(i, carry):
        load(i).wait()
        p, x = lax.div(i, 4), lax.rem(i, 4)
        probe = jnp.zeros((SEQ, 128), F32)
        for zh in range(4):
            here = pl.ds(pl.multiple_of(x * 1024 + zh * 256, 256), 256)
            cur = in_buf[i, :, zh * 256 : (zh + 1) * 256].astype(F32)
            shifted = jnp.where(row == 0, 0.0, pltpu.roll(cur, 1, 0))
            mixed = (cur + (shifted - cur) * mix_ref[0:1, here]).astype(BF)
            prod = mixed.astype(F32) * left_ref[pl.ds(p, 1), here]
            probe = probe + prod[:, :128] + prod[:, 128:]
            out_buf[i, zh, 0] = mixed[:, :128]
            out_buf[i, zh, 1] = mixed[:, 128:]
        probe_ref[p] += probe
        for copy in save(i):
            copy.start()
        return carry

    lax.fori_loop(0, 8, one, 0)
    for i in range(8):
        for copy in save(i):
            copy.wait()


def mix(scalars, inputs, mix_key, key_left, tokens=()):
    return call(
        mix_kernel,
        "mix",
        [inputs, mix_key.reshape(1, D), key_left.astype(F32)],
        [ANY, whole((1, D)), whole((2, D))],
        [array((4, 4, 2 * SEQ, 128), BF)] * 2 + [array((2, SEQ, 128), F32)],
        [ANY, ANY, whole((2, SEQ, 128))],
        scalars=scalars,
        tokens=tokens,
        scratch=[
            pltpu.VMEM((8, SEQ, 1024), BF),
            pltpu.VMEM((8, 4, 2, SEQ, 128), BF),
            pltpu.SemaphoreType.DMA((8,)),
            pltpu.SemaphoreType.DMA((8, 2)),
        ],
        us=16,
    )


def gather(pieces, places, buf_ref, sems):
    loads = [
        pltpu.make_async_copy(ref, buf_ref.at[i], sems.at[i, 0]) for i, ref in enumerate(pieces)
    ]
    saves = [
        pltpu.make_async_copy(buf_ref.at[i], ref, sems.at[i, 1]) for i, ref in enumerate(places)
    ]
    for load in loads:
        load.start()
    for load, save in zip(loads, saves):
        load.wait()
        save.start()
    for save in saves:
        save.wait()


def join_kernel(*refs):
    out_ref, buf_ref, sems = refs[-3:]
    places = [out_ref.at[i * 128 : (i + 1) * 128] for i in range(3)]
    gather(refs[:3], places, buf_ref, sems)


def join(blocks, tokens):
    return call(
        join_kernel,
        "join",
        blocks,
        [ANY] * 3,
        array((384, 1024), BF),
        ANY,
        tokens=tokens,
        scratch=[pltpu.VMEM((3, 128, 1024), BF), pltpu.SemaphoreType.DMA((3, 2))],
        us=4,
    )


BACK = (1, 3, 2)


def both_kernel(s_ref, mine_ref, got_ref, *refs):
    own, rest, refs = refs[:4], refs[4:7], refs[7:]
    own_ref, other_ref, w_ref, in_ref, own_buf, other_buf, sems = refs
    x, zh, way = s_ref[0], s_ref[1], 2 * s_ref[2] - 1
    places = [(0, k) for k in range(4)] + [(back, k) for k in (0, 1, 3) for back in BACK]

    def rows(half, ref):
        copies = []
        for i, (back, k) in enumerate(places):
            at = lax.rem(zh + way * back + 4, 4)
            col = lax.rem(x + way * k + 4, 4)
            copies.append(
                pltpu.make_async_copy(
                    ref.at[at, col],
                    in_ref.at[half, :, i * 128 : i * 128 + 128],
                    sems.at[i, half],
                )
            )
        return copies

    weights = [
        pltpu.make_async_copy(own[k], w_ref.at[k * 128 : k * 128 + 128], sems.at[k, 2])
        for k in range(4)
    ]
    for k in range(3):
        row = 512 + k * 384
        weights.append(
            pltpu.make_async_copy(rest[k], w_ref.at[row : row + 384], sems.at[4 + k, 2])
        )
    first, second = rows(1, got_ref), rows(0, mine_ref)
    for copy in weights + first + second:
        copy.start()
    for copy in weights + first:
        copy.wait()
    other_buf[...] = jnp.dot(in_ref[1], w_ref[...], preferred_element_type=F32).astype(BF)
    save = pltpu.make_async_copy(other_buf, other_ref, sems.at[7, 2])
    save.start()
    for copy in second:
        copy.wait()
    saves = [save]
    for n in range(2):
        cols = slice(n * 512, n * 512 + 512)
        own_buf[n] = jnp.dot(in_ref[0], w_ref[:, cols], preferred_element_type=F32)
        save = pltpu.make_async_copy(own_buf.at[n], own_ref.at[n], sems.at[8 + n, 2])
        save.start()
        saves.append(save)
    for save in saves:
        save.wait()


def both_step(scalars, mine, got, own, rest, tokens=()):
    return call(
        both_kernel,
        "both",
        [mine, got, *own, *rest],
        [ANY] * 9,
        [array((2, 2 * SEQ, 512), F32), array((2 * SEQ, 1024), BF)],
        [ANY] * 2,
        scalars=scalars,
        tokens=tokens,
        scratch=[
            pltpu.VMEM((1664, 1024), BF),
            pltpu.VMEM((2, 512, 1664), BF),
            pltpu.VMEM((2, 512, 512), F32),
            pltpu.VMEM((512, 1024), BF),
            pltpu.SemaphoreType.DMA((13, 3)),
        ],
        us=24,
    )


def last_kernel(s_ref, mine_ref, its_ref, acc_ref, got_ref, right_ref, left_ref, *refs):
    blocks, (out_ref, w_ref, in_ref, acc_buf, got_buf, out_buf, sems) = refs[:2], refs[2:]
    x, zh, way = s_ref[0], s_ref[1], 2 * s_ref[2] - 1
    far = lax.rem(x + 2, 4)
    copies = []
    for half, (sign, ref) in enumerate(((way, mine_ref), (-way, its_ref))):
        row = half * 384
        copies.append(
            pltpu.make_async_copy(blocks[half], w_ref.at[row : row + 384], sems.at[half, 3])
        )
        for i, back in enumerate(BACK):
            at = lax.rem(zh + sign * back + 4, 4)
            col = row + i * 128
            copies.append(
                pltpu.make_async_copy(
                    ref.at[at, far], in_ref.at[:, col : col + 128], sems.at[half, i]
                )
            )
    sums = [
        pltpu.make_async_copy(got_ref, got_buf, sems.at[0, 4]),
        pltpu.make_async_copy(acc_ref, acc_buf, sems.at[1, 4]),
    ]
    for copy in copies + sums:
        copy.start()
    for copy in copies:
        copy.wait()
    row = lax.broadcasted_iota(jnp.int32, (16, 1024), 0)
    saves = []
    for p in range(2):
        rows = slice(p * SEQ, (p + 1) * SEQ)
        total = jnp.dot(in_ref[rows], w_ref[...], preferred_element_type=F32)
        if p == 0:
            for copy in sums:
                copy.wait()
        total = total + got_buf[rows].astype(F32)
        for n in range(2):
            cols = slice(n * 512, n * 512 + 512)
            out_buf[p, :SEQ, cols] = (total[:, cols] + acc_buf[n, rows]).astype(BF)
        tail = jnp.where(row == 1, left_ref[p : p + 1], 0.0)
        out_buf[p, SEQ:] = jnp.where(row == 0, right_ref[p : p + 1], tail).astype(BF)
        save = pltpu.make_async_copy(out_buf.at[p], out_ref.at[p], sems.at[p, 5])
        save.start()
        saves.append(save)
    for save in saves:
        save.wait()


def last_step(scalars, mine, its, acc, got, right, left, blocks, tokens=()):
    return call(
        last_kernel,
        "last",
        [mine, its, acc, got, right, left, *blocks],
        [ANY] * 4 + [whole((2, 1024))] * 2 + [ANY] * 2,
        array((2, SEQ + 16, 1024), BF),
        ANY,
        scalars=scalars,
        tokens=tokens,
        scratch=[
            pltpu.VMEM((768, 1024), BF),
            pltpu.VMEM((512, 768), BF),
            pltpu.VMEM((2, 512, 512), F32),
            pltpu.VMEM((512, 1024), BF),
            pltpu.VMEM((2, SEQ + 16, 1024), BF),
            pltpu.SemaphoreType.DMA((2, 6)),
        ],
        us=16,
    )


def order_kernel(s_ref, *refs):
    out_ref, buf_ref, sems = refs[4:]
    gather(refs[:4], [out_ref.at[s_ref[k]] for k in range(4)], buf_ref, sems)


def order(scalars, pieces, tokens=()):
    return call(
        order_kernel,
        "order",
        pieces,
        [ANY] * 4,
        array((4, 1024, 128), BF),
        ANY,
        scalars=scalars,
        tokens=tokens,
        scratch=[pltpu.VMEM((4, 1024, 128), BF), pltpu.SemaphoreType.DMA((4, 2))],
        us=4,
    )


def value_copies(s_ref, own, other, first, w_ref, sems):
    x, c = s_ref[0], s_ref[1]
    copies = []
    for k in range(4):
        for half, blocks in enumerate((own, other)):
            core = c if half == 0 else 1 - c
            at = lax.rem(x + (2 * core - 1) * k + 4, 4)
            for n in range(2):
                col = pl.multiple_of(core * 128 + n * 256, 128)
                copy = pltpu.make_async_copy(
                    blocks[k].at[first + n],
                    w_ref.at[at, :, pl.ds(col, 128)],
                    sems.at[k, half, n],
                )
                copy.start()
                copies.append(copy)
    return copies


def add_side(total, side_ref, right_ref, out_ref):
    for n in range(4):
        cols = slice(n * 128, (n + 1) * 128)
        out = total[:, cols] + side_ref[...] * right_ref[:, cols]
        out_ref[:, cols] = out.astype(out_ref.dtype)


def send_kernel(pair, s_ref, b0, b1, b2, b3, probe_ref, right_ref, *refs):
    own, other, refs = refs[:4], refs[4:8], refs[8:]
    out_ref, h_out, side_ref, b_ref, h_ref, w_ref, h_sems, sems = refs
    loads = [
        pltpu.make_async_copy(base.at[pair], b_ref.at[k], h_sems.at[4 + k])
        for k, base in enumerate((b0, b1, b2, b3))
    ]
    loads[0].start()
    copies = value_copies(s_ref, own, other, 0, w_ref, sems)
    for load in loads[1:]:
        load.start()
    y, way, sign = s_ref[2], 2 * s_ref[1] - 1, s_ref[3].astype(F32)
    probe_all = jnp.sum(probe_ref[0], axis=1, keepdims=True) * (0.5 * sign / math.sqrt(D))
    side_ref[...] = jnp.zeros_like(side_ref)

    def hide(k):
        loads[k].wait()
        vecs = b_ref[k, SEQ:, :].astype(F32)
        for lo in range(0, SEQ, 128):
            rows = slice(lo, lo + 128)
            side = [jnp.zeros((128, 128), F32), jnp.zeros((128, 128), F32)]
            for col in range(0, 1024, 256):
                cols = slice(col, col + 256)
                act = b_ref[k, rows, cols].astype(F32)
                nudge = probe_all[rows] * vecs[0:1, cols]
                left = vecs[1:2, cols]
                for m, pre in enumerate((act + nudge, act - nudge)):
                    pre = jnp.maximum(pre, 0.0)
                    square = pre * pre
                    h_ref[k, m * SEQ + lo : m * SEQ + lo + 128, cols] = square.astype(BF)
                    prod = square * left
                    side[m] = side[m] + prod[:, :128] + prod[:, 128:]
            for m in range(2):
                side_ref[m * SEQ + lo : m * SEQ + lo + 128, :] += side[m]
        save = pltpu.make_async_copy(h_ref.at[k], h_out.at[k], h_sems.at[k])
        save.start()
        return save

    saves = [hide(k) for k in range(4)]
    for copy in copies:
        copy.wait()
    total = None
    for k in range(4):
        at = lax.rem(y + way * k + 4, 4)
        part = jnp.dot(h_ref[k], w_ref[at], preferred_element_type=F32)
        total = part if total is None else total + part
    scale = 0.5 / math.sqrt(FF) * sign
    for m in range(2):
        rows = slice(m * SEQ, (m + 1) * SEQ)
        side = jnp.sum(side_ref[rows, :], axis=1, keepdims=True) * (scale if m == 0 else -scale)
        side_ref[rows, :] = jnp.broadcast_to(side, (SEQ, 128))
    add_side(total, side_ref, right_ref, out_ref)
    for save in saves:
        save.wait()


def send_step(scalars, base, probe, pair, right, own, other, tokens=()):
    return call(
        functools.partial(send_kernel, pair),
        "send",
        [*base, probe, right, *own, *other],
        [ANY] * 4
        + [pl.BlockSpec((1, SEQ, 128), lambda i, s: (pair, 0, 0)), whole((1, 512))]
        + [ANY] * 8,
        [
            array((2 * SEQ, 512), BF),
            array((4, 2 * SEQ, 1024), BF),
            array((2 * SEQ, 128), F32),
        ],
        [whole((2 * SEQ, 512)), ANY, whole((2 * SEQ, 128))],
        scalars=scalars,
        tokens=tokens,
        scratch=[
            pltpu.VMEM((4, SEQ + 16, 1024), BF),
            pltpu.VMEM((4, 2 * SEQ, 1024), BF),
            pltpu.VMEM((4, 1024, 512), BF),
            pltpu.SemaphoreType.DMA((8,)),
            pltpu.SemaphoreType.DMA((4, 2, 2)),
        ],
        us=16,
    )


def keep_kernel(s_ref, h0, h1, side0, side1, right_ref, *refs):
    own, other, refs = refs[:4], refs[4:8], refs[8:]
    out0, out1, h_ref, w_ref, out_buf, h_sems, sems = refs
    loads = [
        [pltpu.make_async_copy(h.at[k], h_ref.at[p, k], h_sems.at[p, k]) for k in range(4)]
        for p, h in enumerate((h0, h1))
    ]
    loads[0][0].start()
    copies = value_copies(s_ref, own, other, 2, w_ref, sems)
    for load in loads[0][1:] + loads[1]:
        load.start()
    y, way = s_ref[2], 2 * s_ref[1] - 1
    for copy in copies:
        copy.wait()
    saves = []
    for p, (side_ref, out_ref) in enumerate(((side0, out0), (side1, out1))):
        total = None
        for k in range(4):
            loads[p][k].wait()
            at = lax.rem(y + way * k + 4, 4)
            part = jnp.dot(h_ref[p, k], w_ref[at], preferred_element_type=F32)
            total = part if total is None else total + part
        add_side(total, side_ref, right_ref.at[p : p + 1], out_buf.at[p])
        save = pltpu.make_async_copy(out_buf.at[p], out_ref, h_sems.at[p, 4])
        save.start()
        saves.append(save)
    for save in saves:
        save.wait()


def keep_step(scalars, hidden, side, right, own, other, tokens=()):
    return call(
        keep_kernel,
        "keep",
        [*hidden, *side, right, *own, *other],
        [ANY] * 2 + [whole((2 * SEQ, 128))] * 2 + [whole((2, 512))] + [ANY] * 8,
        [array((2 * SEQ, 512), F32)] * 2,
        [ANY] * 2,
        scalars=scalars,
        tokens=tokens,
        scratch=[
            pltpu.VMEM((2, 4, 2 * SEQ, 1024), BF),
            pltpu.VMEM((4, 1024, 512), BF),
            pltpu.VMEM((2, 2 * SEQ, 512), F32),
            pltpu.SemaphoreType.DMA((2, 5)),
            pltpu.SemaphoreType.DMA((4, 2, 2)),
        ],
        us=16,
    )


def finish_kernel(pair, s_ref, *refs):
    if pair == 1:
        refs = refs[1:]
    keep_ref, got_ref, target_ref, out_ref, err_ref = refs
    target = target_ref[0].astype(F32)
    lane = lax.broadcasted_iota(jnp.int32, (1, 128), 1)
    errs = jnp.zeros((1, 128), F32)
    for m in range(2):
        rows = slice(m * SEQ, (m + 1) * SEQ)
        out = (keep_ref[rows, :] + got_ref[rows, :].astype(F32)).astype(BF)
        out_ref[m] = out
        gap = out.astype(F32) - target
        err = jnp.sum(gap * gap)
        errs = errs + jnp.where(lane == 4 * s_ref[0] + 2 * pair + m, err, 0.0)
    err_ref[...] = errs


def finish(scalars, pair, keep, got, targets, outputs=None):
    args = [] if outputs is None else [outputs]
    return pl.pallas_call(
        functools.partial(finish_kernel, pair),
        grid_spec=pltpu.PrefetchScalarGridSpec(
            num_scalar_prefetch=1,
            grid=(1,),
            in_specs=[ANY] * len(args)
            + [whole((2 * SEQ, 512))] * 2
            + [pl.BlockSpec((1, SEQ, 512), lambda i, s: (pair, 0, 0))],
            out_specs=[pl.BlockSpec((2, SEQ, 512), lambda i, s: (pair, 0, 0)), whole((1, 128))],
        ),
        out_shape=[array((4, SEQ, 512), BF), array((1, 128), F32)],
        input_output_aliases={1: 0} if args else {},
        compiler_params=pltpu.CompilerParams(vmem_limit_bytes=56 * 2**20),
        cost_estimate=pl.CostEstimate(flops=2**31, bytes_accessed=2**20, transcendentals=0),
        name="finish",
    )(scalars, *args, keep, got, targets)


def outer(left, right):
    high = left.astype(BF)
    low = (left - high.astype(F32)).astype(BF)
    left = jnp.concatenate([high, low], 0)
    right = jnp.concatenate([right, right], 0)
    return lax.dot_general(left, right, (((0,), (0,)), ((), ())), preferred_element_type=F32)


def update_kernel(err_ref, lk_ref, rk_ref, lv_ref, rv_ref, key_ref, value_ref):
    err = jnp.sum(err_ref[...], axis=1) / (SEQ * D)
    lane = lax.broadcasted_iota(jnp.int32, err.shape, 1)
    used = lane < 8
    mean = jnp.sum(jnp.where(used, err, 0.0)) / 128
    var = jnp.sum(jnp.where(used, (err - mean) * (err - mean), 0.0)) / 128
    spread = jnp.sqrt(jnp.full((1, 1), var + 1e-05, F32))
    diff = err - pltpu.roll(err, 127, 1)
    coef = jnp.concatenate([diff[:, i : i + 1] for i in (0, 2, 4, 6)], 0) / (spread * math.sqrt(64))
    key_ref[...] = outer(lk_ref[...].astype(F32) * coef, rk_ref[...])
    value_ref[...] = outer(lv_ref[...].astype(F32) * coef, rv_ref[...])


def update(err, left_key, right_key, left_value, right_value):
    args = [err, left_key, right_key, left_value, right_value]
    return call(
        update_kernel,
        "update",
        args,
        [whole(v.shape) for v in args],
        [array((128, 1024), F32), array((1024, 128), F32)],
        [whole((128, 1024)), whole((1024, 128))],
    )


def per_device(
    inputs,
    mix_key,
    key_weight,
    value_weight,
    key_left,
    key_right,
    value_left,
    value_right,
    pair_sign,
    targets,
):
    pop, mp = lax.axis_index("pop"), lax.axis_index("mp")
    x, zh, c = pop // 8, (pop // 2) % 4, pop % 2
    y, zl = mp // 2, mp % 2
    i32 = lambda *v: jnp.stack([jnp.asarray(e, jnp.int32) for e in v])

    def swap(values):
        return [move(v, c=1) for v in values]

    own_x = [key_weight, step(key_weight, "x"), None, step(key_weight, "x", -1)]
    key_z = [step(key_weight, "zh"), step(key_weight, "zh", -1), None]
    moved = transpose_xy(value_weight)
    mine, its, probe = mix(i32(c), inputs, mix_key, key_left, [own_x[1]])
    own_x[1], key_z[0] = fence([own_x[1], key_z[0]], [own_x[3], key_z[1], moved, probe])
    own_x[2], key_z[2] = step(own_x[1], "x"), step(key_z[0], "zh")
    rest = join(key_z, [own_x[2]])
    rest = [rest, step(rest, "x"), None, step(rest, "x", -1)]
    value_z = [moved, step(moved, "zh"), None, step(moved, "zh", -1)]
    rest[1], value_z[1] = fence([rest[1], value_z[1]], [rest[3], value_z[3]])
    rest[2], value_z[2] = step(rest[1], "x"), step(value_z[1], "zh")
    me = i32(x, zh, c)
    got = move(its, c=1)
    acc, other = both_step(me, mine, got, own_x, [rest[0], rest[1], rest[3]])
    (other,) = fence([other], [value_z[2]])
    got = move(other, c=1)
    vecs = [key_right.astype(F32), value_left.astype(F32)]
    base = last_step(me, mine, its, acc, got, *vecs, [rest[2], move(rest[2], c=1)])

    slots = [(zh + (2 * c - 1) * k) % 4 for k in range(4)]
    slots = i32(*[jnp.where(s // 2 == zl, 2, 0) + s % 2 for s in slots])
    value_x = order(slots, value_z)
    (value_x,) = fence([value_x], [base])
    value_x = [value_x, step(value_x, "x"), None, step(value_x, "x", -1)]
    value_w = [move(value_x[0], c=1)]
    near = [base, step(base, "y"), None, step(base, "y", -1)]

    def to_owner(v):
        return v.reshape(2, 32, 128).transpose(1, 0, 2)

    def to_all(v):
        return jnp.broadcast_to(v.reshape(1, 16, 128), (32, 16, 128))

    sign = pair_sign.astype(BF)[:, None]
    parcel = jnp.concatenate(
        [
            to_owner(key_left * sign),
            to_owner(value_right),
            to_all(key_right),
            to_all(value_left * sign),
        ],
        1,
    )
    (parcel,) = fence([parcel], [base])
    parcel = lax.all_to_all(parcel, "pop", split_axis=0, concat_axis=0, tiled=True)

    def unpack(lo, hi):
        v = parcel[:, lo:hi].reshape(16, 2, 2, (hi - lo) // 2 * 128)
        return v.transpose(1, 2, 0, 3).reshape(64, (hi - lo) // 2 * 128)

    left_key, right_value = unpack(0, 2), unpack(2, 4)
    right_key, left_value = unpack(4, 20), unpack(20, 36)
    right = value_right.astype(F32)
    send_right, keep_right = (
        lax.dynamic_slice_in_dim(right, (2 * y + half) * 512, 512, 1) for half in (1 - zl, zl)
    )
    at = [i32(x, c, y, pair_sign[p]) for p in range(2)]
    value_x[1], near[1] = fence(
        [value_x[1], near[1]], [value_x[3], near[3], parcel, send_right, keep_right, *at]
    )
    value_x[2], near[2] = step(value_x[1], "x"), step(near[1], "y")
    value_w = (value_x, value_w + swap(value_x[1:]))

    hidden, got = [], []
    for p in range(2):
        send, *hid = send_step(at[p], near, probe, p, send_right[p : p + 1], *value_w)
        hidden.append((send, *hid))
        got.append(move(send, zl=1))
    sends, hids, sides = zip(*hidden)
    keep = keep_step(at[0], hids, sides, keep_right, *value_w, sends)
    outputs, err0 = finish(i32(c), 0, keep[0], got[0], targets)
    outputs, err1 = finish(i32(c), 1, keep[1], got[1], targets, outputs)
    err = err0 + err1

    err = err + move(err, c=1)
    err = jnp.broadcast_to(err[None], (128, 1, 128))
    groups = [[place(at["x"], at["zh"], core, at["y"], at["zl"]) for at in everywhere() if at["c"] == core] for core in range(2)]
    err = lax.all_to_all(
        err, AXES, split_axis=0, concat_axis=0, tiled=True, axis_index_groups=groups
    )
    key_update, value_update = update(
        err.reshape(16, 8, 128), left_key, right_key, left_value, right_value
    )
    return outputs, key_update, value_update


def solution(mesh):
    in_specs = (
        P("pop", None, None),
        P(),
        P("pop", "mp"),
        P("mp", "pop"),
        P("pop", None),
        P("pop", "mp"),
        P("pop", "mp"),
        P("pop", None),
        P("pop"),
        P("pop", None, "mp"),
    )
    out_specs = (P("pop", None, "mp"), P("pop", "mp"), P("mp", "pop"))
    return jax.shard_map(
        per_device, mesh=mesh, in_specs=in_specs, out_specs=out_specs, check_vma=False
    )
```

```python
import functools
import math

import jax
import jax.numpy as jnp
from jax import lax
from jax.experimental import pallas as pl
from jax.experimental.pallas import tpu as pltpu
from jax.sharding import PartitionSpec as P

FF = 8192
D = 4096
SEQ = 256
BF = jnp.bfloat16
F32 = jnp.float32
AXES = ("pop", "mp")
SIZES = dict(x=4, zh=4, c=2, y=4, zl=2)


def place(x, zh, c, y, zl):
    return ((x * 4 + zh) * 2 + c) * 8 + y * 2 + zl


def everywhere():
    for x in range(4):
        for zh in range(4):
            for c in range(2):
                for y in range(4):
                    for zl in range(2):
                        yield dict(x=x, zh=zh, c=c, y=y, zl=zl)


def move(value, **shift):
    pairs = []
    for at in everywhere():
        to = {k: (v + shift.get(k, 0)) % SIZES[k] for k, v in at.items()}
        pairs.append((place(**at), place(**to)))
    return lax.ppermute(value, AXES, pairs)


def step(value, axis, way=1):
    pairs = []
    for at in everywhere():
        to = {**at, axis: (at[axis] + way * (1 - 2 * at["c"])) % SIZES[axis]}
        pairs.append((place(**at), place(**to)))
    return lax.ppermute(value, AXES, pairs)


def ring(value, axis):
    back = step(value, axis)
    return [value, back, step(back, axis), step(value, axis, -1)]


def transpose_xy(value):
    pairs = []
    for at in everywhere():
        pairs.append((place(**at), place(**{**at, "x": at["y"], "y": at["x"]})))
    return lax.ppermute(value, AXES, pairs)


ANY = pl.BlockSpec(memory_space=pltpu.HBM)


def whole(shape):
    return pl.BlockSpec(shape, lambda *_: (0,) * len(shape))


def call(kernel, name, args, specs, outs, out_specs, *, grid=(1,), scalars=None, tokens=(), scratch=(), us=1):
    lead = 0 if scalars is None else 1

    def body(*refs):
        kernel(*refs[:lead], *refs[lead + len(tokens) :])

    return pl.pallas_call(
        body,
        grid_spec=pltpu.PrefetchScalarGridSpec(
            num_scalar_prefetch=lead,
            grid=grid,
            in_specs=[ANY] * len(tokens) + list(specs),
            out_specs=out_specs,
            scratch_shapes=list(scratch),
        ),
        out_shape=outs,
        compiler_params=pltpu.CompilerParams(vmem_limit_bytes=63 * 2**20),
        cost_estimate=pl.CostEstimate(flops=us * 2**30, bytes_accessed=2**20, transcendentals=0),
        name=name,
    )(*([scalars] if lead else []), *tokens, *args)


def array(shape, dtype):
    return jax.ShapeDtypeStruct(shape, dtype)


def fence(values, tokens=()):
    count = len(values)
    return pl.pallas_call(
        lambda *refs: None,
        in_specs=[ANY] * (count + len(tokens)),
        out_specs=[ANY] * count,
        out_shape=[array(v.shape, v.dtype) for v in values],
        input_output_aliases={i: i for i in range(count)},
        compiler_params=pltpu.CompilerParams(vmem_limit_bytes=63 * 2**20),
        name="fence",
    )(*values, *tokens)


def mix_kernel(
    s_ref, x_ref, mix_ref, left_ref, mine_ref, its_ref, probe_ref, in_buf, out_buf, in_sems, out_sems
):
    def load(i):
        p, x = lax.div(i, 4), lax.rem(i, 4)
        return pltpu.make_async_copy(
            x_ref.at[p, :, pl.ds(pl.multiple_of(x * 1024, 1024), 1024)], in_buf.at[i], in_sems.at[i]
        )

    def save(i):
        p, x = lax.div(i, 4), lax.rem(i, 4)
        rows = pl.ds(pl.multiple_of(p * SEQ, SEQ), SEQ)
        return [
            pltpu.make_async_copy(
                out_buf.at[i, :, core], ref.at[:, x, rows], out_sems.at[i, half]
            )
            for half, (core, ref) in enumerate(((s_ref[0], mine_ref), (1 - s_ref[0], its_ref)))
        ]

    for i in range(8):
        load(i).start()
    probe_ref[...] = jnp.zeros_like(probe_ref)
    row = lax.broadcasted_iota(jnp.int32, (SEQ, 256), 0)

    def one(i, carry):
        load(i).wait()
        p, x = lax.div(i, 4), lax.rem(i, 4)
        probe = jnp.zeros((SEQ, 128), F32)
        for zh in range(4):
            here = pl.ds(pl.multiple_of(x * 1024 + zh * 256, 256), 256)
            cur = in_buf[i, :, zh * 256 : (zh + 1) * 256].astype(F32)
            shifted = jnp.where(row == 0, 0.0, pltpu.roll(cur, 1, 0))
            mixed = (cur + (shifted - cur) * mix_ref[0:1, here]).astype(BF)
            left = jnp.where(p == 0, left_ref[0:1, here], left_ref[1:2, here]).astype(F32)
            prod = mixed.astype(F32) * left
            probe = probe + prod[:, :128] + prod[:, 128:]
            out_buf[i, zh, 0] = mixed[:, :128]
            out_buf[i, zh, 1] = mixed[:, 128:]
        probe_ref[p] += probe
        for copy in save(i):
            copy.start()
        return carry

    lax.fori_loop(0, 8, one, 0)
    for i in range(8):
        for copy in save(i):
            copy.wait()


def mix(scalars, inputs, mix_key, key_left, tokens=()):
    return call(
        mix_kernel,
        "mix",
        [inputs, mix_key.reshape(1, D), key_left],
        [ANY, whole((1, D)), whole((2, D))],
        [array((4, 4, 2 * SEQ, 128), BF)] * 2 + [array((2, SEQ, 128), F32)],
        [ANY, ANY, whole((2, SEQ, 128))],
        scalars=scalars,
        tokens=tokens,
        scratch=[
            pltpu.VMEM((8, SEQ, 1024), BF),
            pltpu.VMEM((8, 4, 2, SEQ, 128), BF),
            pltpu.SemaphoreType.DMA((8,)),
            pltpu.SemaphoreType.DMA((8, 2)),
        ],
        us=16,
    )


def gather(pieces, places, buf_ref, sems):
    loads = [
        pltpu.make_async_copy(ref, buf_ref.at[i], sems.at[i, 0]) for i, ref in enumerate(pieces)
    ]
    saves = [
        pltpu.make_async_copy(buf_ref.at[i], ref, sems.at[i, 1]) for i, ref in enumerate(places)
    ]
    for load in loads:
        load.start()
    for load, save in zip(loads, saves):
        load.wait()
        save.start()
    for save in saves:
        save.wait()


def join_kernel(*refs):
    out_ref, buf_ref, sems = refs[-3:]
    places = [out_ref.at[i * 128 : (i + 1) * 128] for i in range(3)]
    gather(refs[:3], places, buf_ref, sems)


def join(blocks, tokens):
    return call(
        join_kernel,
        "join",
        blocks,
        [ANY] * 3,
        array((384, 1024), BF),
        ANY,
        tokens=tokens,
        scratch=[pltpu.VMEM((3, 128, 1024), BF), pltpu.SemaphoreType.DMA((3, 2))],
        us=4,
    )


BACK = (1, 3, 2)


def both_kernel(s_ref, mine_ref, got_ref, *refs):
    own, rest, refs = refs[:4], refs[4:7], refs[7:]
    own_ref, other_ref, w_ref, in_ref, own_buf, other_buf, sems = refs
    x, zh, way = s_ref[0], s_ref[1], 2 * s_ref[2] - 1
    places = [(0, k) for k in range(4)] + [(back, k) for k in (0, 1, 3) for back in BACK]

    def rows(half, ref):
        copies = []
        for i, (back, k) in enumerate(places):
            at = lax.rem(zh + way * back + 4, 4)
            col = lax.rem(x + way * k + 4, 4)
            copies.append(
                pltpu.make_async_copy(
                    ref.at[at, col],
                    in_ref.at[half, :, i * 128 : i * 128 + 128],
                    sems.at[i, half],
                )
            )
        return copies

    weights = [
        pltpu.make_async_copy(own[k], w_ref.at[k * 128 : k * 128 + 128], sems.at[k, 2])
        for k in range(4)
    ]
    for k in range(3):
        row = 512 + k * 384
        weights.append(
            pltpu.make_async_copy(rest[k], w_ref.at[row : row + 384], sems.at[4 + k, 2])
        )
    first, second = rows(1, got_ref), rows(0, mine_ref)
    for copy in weights + first + second:
        copy.start()
    for copy in weights + first:
        copy.wait()
    other_buf[...] = jnp.dot(in_ref[1], w_ref[...], preferred_element_type=F32).astype(BF)
    save = pltpu.make_async_copy(other_buf, other_ref, sems.at[7, 2])
    save.start()
    for copy in second:
        copy.wait()
    saves = [save]
    for n in range(2):
        cols = slice(n * 512, n * 512 + 512)
        own_buf[n] = jnp.dot(in_ref[0], w_ref[:, cols], preferred_element_type=F32)
        save = pltpu.make_async_copy(own_buf.at[n], own_ref.at[n], sems.at[8 + n, 2])
        save.start()
        saves.append(save)
    for save in saves:
        save.wait()


def both_step(scalars, mine, got, own, rest, tokens=()):
    return call(
        both_kernel,
        "both",
        [mine, got, *own, *rest],
        [ANY] * 9,
        [array((2, 2 * SEQ, 512), F32), array((2 * SEQ, 1024), BF)],
        [ANY] * 2,
        scalars=scalars,
        tokens=tokens,
        scratch=[
            pltpu.VMEM((1664, 1024), BF),
            pltpu.VMEM((2, 512, 1664), BF),
            pltpu.VMEM((2, 512, 512), F32),
            pltpu.VMEM((512, 1024), BF),
            pltpu.SemaphoreType.DMA((13, 3)),
        ],
        us=24,
    )


def last_kernel(s_ref, mine_ref, its_ref, acc_ref, got_ref, right_ref, left_ref, *refs):
    blocks, (out_ref, w_ref, in_ref, acc_buf, got_buf, out_buf, sems) = refs[:2], refs[2:]
    x, zh, way = s_ref[0], s_ref[1], 2 * s_ref[2] - 1
    far = lax.rem(x + 2, 4)
    copies = []
    for half, (sign, ref) in enumerate(((way, mine_ref), (-way, its_ref))):
        row = half * 384
        copies.append(
            pltpu.make_async_copy(blocks[half], w_ref.at[row : row + 384], sems.at[half, 3])
        )
        for i, back in enumerate(BACK):
            at = lax.rem(zh + sign * back + 4, 4)
            col = row + i * 128
            copies.append(
                pltpu.make_async_copy(
                    ref.at[at, far], in_ref.at[:, col : col + 128], sems.at[half, i]
                )
            )
    sums = [
        pltpu.make_async_copy(got_ref, got_buf, sems.at[0, 4]),
        pltpu.make_async_copy(acc_ref, acc_buf, sems.at[1, 4]),
    ]
    for copy in copies + sums:
        copy.start()
    for copy in copies:
        copy.wait()
    row = lax.broadcasted_iota(jnp.int32, (16, 1024), 0)
    saves = []
    for p in range(2):
        rows = slice(p * SEQ, (p + 1) * SEQ)
        total = jnp.dot(in_ref[rows], w_ref[...], preferred_element_type=F32)
        if p == 0:
            for copy in sums:
                copy.wait()
        total = total + got_buf[rows].astype(F32)
        for n in range(2):
            cols = slice(n * 512, n * 512 + 512)
            out_buf[p, :SEQ, cols] = (total[:, cols] + acc_buf[n, rows]).astype(BF)
        tail = jnp.where(row == 1, left_ref[p : p + 1], 0.0)
        out_buf[p, SEQ:] = jnp.where(row == 0, right_ref[p : p + 1], tail).astype(BF)
        save = pltpu.make_async_copy(out_buf.at[p], out_ref.at[p], sems.at[p, 5])
        save.start()
        saves.append(save)
    for save in saves:
        save.wait()


def last_step(scalars, mine, its, acc, got, right, left, blocks, tokens=()):
    return call(
        last_kernel,
        "last",
        [mine, its, acc, got, right, left, *blocks],
        [ANY] * 4 + [whole((2, 1024))] * 2 + [ANY] * 2,
        array((2, SEQ + 16, 1024), BF),
        ANY,
        scalars=scalars,
        tokens=tokens,
        scratch=[
            pltpu.VMEM((768, 1024), BF),
            pltpu.VMEM((512, 768), BF),
            pltpu.VMEM((2, 512, 512), F32),
            pltpu.VMEM((512, 1024), BF),
            pltpu.VMEM((2, SEQ + 16, 1024), BF),
            pltpu.SemaphoreType.DMA((2, 6)),
        ],
        us=16,
    )


def order_kernel(s_ref, *refs):
    out_ref, buf_ref, sems = refs[4:]
    gather(refs[:4], [out_ref.at[s_ref[k]] for k in range(4)], buf_ref, sems)


def order(scalars, pieces, tokens=()):
    return call(
        order_kernel,
        "order",
        pieces,
        [ANY] * 4,
        array((4, 1024, 128), BF),
        ANY,
        scalars=scalars,
        tokens=tokens,
        scratch=[pltpu.VMEM((4, 1024, 128), BF), pltpu.SemaphoreType.DMA((4, 2))],
        us=4,
    )


def value_copies(s_ref, own, other, first, w_ref, sems):
    x, c = s_ref[0], s_ref[1]
    copies = []
    for k in range(4):
        for half, blocks in enumerate((own, other)):
            core = c if half == 0 else 1 - c
            at = lax.rem(x + (2 * core - 1) * k + 4, 4)
            for n in range(2):
                col = pl.multiple_of(core * 128 + n * 256, 128)
                copy = pltpu.make_async_copy(
                    blocks[k].at[first + n],
                    w_ref.at[at, :, pl.ds(col, 128)],
                    sems.at[k, half, n],
                )
                copy.start()
                copies.append(copy)
    return copies


def add_side(total, side_ref, right_ref, out_ref):
    for n in range(4):
        cols = slice(n * 128, (n + 1) * 128)
        out = total[:, cols] + side_ref[...] * right_ref[:, cols]
        out_ref[:, cols] = out.astype(out_ref.dtype)


def send_kernel(pair, s_ref, b0, b1, b2, b3, probe_ref, right_ref, *refs):
    own, other, refs = refs[:4], refs[4:8], refs[8:]
    out_ref, h_out, side_ref, b_ref, h_ref, w_ref, h_sems, sems = refs
    loads = [
        pltpu.make_async_copy(base.at[pair], b_ref.at[k], h_sems.at[4 + k])
        for k, base in enumerate((b0, b1, b2, b3))
    ]
    loads[0].start()
    copies = value_copies(s_ref, own, other, 0, w_ref, sems)
    for load in loads[1:]:
        load.start()
    y, way, sign = s_ref[2], 2 * s_ref[1] - 1, s_ref[3].astype(F32)
    probe_all = jnp.sum(probe_ref[0], axis=1, keepdims=True) * (0.5 * sign / math.sqrt(D))
    side_ref[...] = jnp.zeros_like(side_ref)

    def hide(k):
        loads[k].wait()
        vecs = b_ref[k, SEQ:, :].astype(F32)
        for lo in range(0, SEQ, 128):
            rows = slice(lo, lo + 128)
            side = [jnp.zeros((128, 128), F32), jnp.zeros((128, 128), F32)]
            for col in range(0, 1024, 256):
                cols = slice(col, col + 256)
                act = b_ref[k, rows, cols].astype(F32)
                nudge = probe_all[rows] * vecs[0:1, cols]
                left = vecs[1:2, cols]
                for m, pre in enumerate((act + nudge, act - nudge)):
                    pre = jnp.maximum(pre, 0.0)
                    square = pre * pre
                    h_ref[k, m * SEQ + lo : m * SEQ + lo + 128, cols] = square.astype(BF)
                    prod = square * left
                    side[m] = side[m] + prod[:, :128] + prod[:, 128:]
            for m in range(2):
                side_ref[m * SEQ + lo : m * SEQ + lo + 128, :] += side[m]
        save = pltpu.make_async_copy(h_ref.at[k], h_out.at[k], h_sems.at[k])
        save.start()
        return save

    saves = [hide(k) for k in range(4)]
    for copy in copies:
        copy.wait()
    total = None
    for k in range(4):
        at = lax.rem(y + way * k + 4, 4)
        part = jnp.dot(h_ref[k], w_ref[at], preferred_element_type=F32)
        total = part if total is None else total + part
    scale = 0.5 / math.sqrt(FF) * sign
    for m in range(2):
        rows = slice(m * SEQ, (m + 1) * SEQ)
        side = jnp.sum(side_ref[rows, :], axis=1, keepdims=True) * (scale if m == 0 else -scale)
        side_ref[rows, :] = jnp.broadcast_to(side, (SEQ, 128))
    add_side(total, side_ref, right_ref.at[pair : pair + 1], out_ref)
    for save in saves:
        save.wait()


def send_step(scalars, base, probe, pair, right, own, other, tokens=()):
    return call(
        functools.partial(send_kernel, pair),
        "send",
        [*base, probe, right, *own, *other],
        [ANY] * 4
        + [pl.BlockSpec((1, SEQ, 128), lambda i, s: (pair, 0, 0)), whole((2, 512))]
        + [ANY] * 8,
        [
            array((2 * SEQ, 512), BF),
            array((4, 2 * SEQ, 1024), BF),
            array((2 * SEQ, 128), F32),
        ],
        [whole((2 * SEQ, 512)), ANY, whole((2 * SEQ, 128))],
        scalars=scalars,
        tokens=tokens,
        scratch=[
            pltpu.VMEM((4, SEQ + 16, 1024), BF),
            pltpu.VMEM((4, 2 * SEQ, 1024), BF),
            pltpu.VMEM((4, 1024, 512), BF),
            pltpu.SemaphoreType.DMA((8,)),
            pltpu.SemaphoreType.DMA((4, 2, 2)),
        ],
        us=16,
    )


def keep_kernel(s_ref, h0, h1, side0, side1, right_ref, *refs):
    own, other, refs = refs[:4], refs[4:8], refs[8:]
    out0, out1, h_ref, w_ref, out_buf, h_sems, sems = refs
    loads = [
        [pltpu.make_async_copy(h.at[k], h_ref.at[p, k], h_sems.at[p, k]) for k in range(4)]
        for p, h in enumerate((h0, h1))
    ]
    loads[0][0].start()
    copies = value_copies(s_ref, own, other, 2, w_ref, sems)
    for load in loads[0][1:] + loads[1]:
        load.start()
    y, way = s_ref[2], 2 * s_ref[1] - 1
    for copy in copies:
        copy.wait()
    saves = []
    for p, (side_ref, out_ref) in enumerate(((side0, out0), (side1, out1))):
        total = None
        for k in range(4):
            loads[p][k].wait()
            at = lax.rem(y + way * k + 4, 4)
            part = jnp.dot(h_ref[p, k], w_ref[at], preferred_element_type=F32)
            total = part if total is None else total + part
        add_side(total, side_ref, right_ref.at[p : p + 1], out_buf.at[p])
        save = pltpu.make_async_copy(out_buf.at[p], out_ref, h_sems.at[p, 4])
        save.start()
        saves.append(save)
    for save in saves:
        save.wait()


def keep_step(scalars, hidden, side, right, own, other, tokens=()):
    return call(
        keep_kernel,
        "keep",
        [*hidden, *side, right, *own, *other],
        [ANY] * 2 + [whole((2 * SEQ, 128))] * 2 + [whole((2, 512))] + [ANY] * 8,
        [array((2 * SEQ, 512), F32)] * 2,
        [ANY] * 2,
        scalars=scalars,
        tokens=tokens,
        scratch=[
            pltpu.VMEM((2, 4, 2 * SEQ, 1024), BF),
            pltpu.VMEM((4, 1024, 512), BF),
            pltpu.VMEM((2, 2 * SEQ, 512), F32),
            pltpu.SemaphoreType.DMA((2, 5)),
            pltpu.SemaphoreType.DMA((4, 2, 2)),
        ],
        us=16,
    )


def finish_kernel(pair, s_ref, *refs):
    errs = jnp.zeros((1, 128), F32)
    if pair == 1:
        errs = refs[1][...]
        refs = refs[2:]
    keep_ref, got_ref, target_ref, out_ref, err_ref = refs
    target = target_ref[0].astype(F32)
    lane = lax.broadcasted_iota(jnp.int32, (1, 128), 1)
    for m in range(2):
        rows = slice(m * SEQ, (m + 1) * SEQ)
        out = (keep_ref[rows, :] + got_ref[rows, :].astype(F32)).astype(BF)
        out_ref[m] = out
        gap = out.astype(F32) - target
        err = jnp.sum(gap * gap)
        errs = errs + jnp.where(lane == 4 * s_ref[0] + 2 * pair + m, err, 0.0)
    err_ref[...] = errs


def finish(scalars, pair, keep, got, targets, done=()):
    return pl.pallas_call(
        functools.partial(finish_kernel, pair),
        grid_spec=pltpu.PrefetchScalarGridSpec(
            num_scalar_prefetch=1,
            grid=(1,),
            in_specs=([ANY, whole((1, 128))] if done else [])
            + [whole((2 * SEQ, 512))] * 2
            + [pl.BlockSpec((1, SEQ, 512), lambda i, s: (pair, 0, 0))],
            out_specs=[pl.BlockSpec((2, SEQ, 512), lambda i, s: (pair, 0, 0)), whole((1, 128))],
        ),
        out_shape=[array((4, SEQ, 512), BF), array((1, 128), F32)],
        input_output_aliases={1: 0} if done else {},
        compiler_params=pltpu.CompilerParams(vmem_limit_bytes=63 * 2**20),
        cost_estimate=pl.CostEstimate(flops=2**31, bytes_accessed=2**20, transcendentals=0),
        name="finish",
    )(scalars, *done, keep, got, targets)


def outer(left, right):
    high = left.astype(BF)
    low = (left - high.astype(F32)).astype(BF)
    left = jnp.concatenate([high, low], 0)
    right = jnp.concatenate([right, right], 0)
    return lax.dot_general(left, right, (((0,), (0,)), ((), ())), preferred_element_type=F32)


def update_kernel(err_ref, lk_ref, rk_ref, lv_ref, rv_ref, key_ref, value_ref):
    err = jnp.sum(err_ref[...], axis=1) / (SEQ * D)
    lane = lax.broadcasted_iota(jnp.int32, err.shape, 1)
    used = lane < 8
    mean = jnp.sum(jnp.where(used, err, 0.0)) / 128
    var = jnp.sum(jnp.where(used, (err - mean) * (err - mean), 0.0)) / 128
    spread = jnp.sqrt(jnp.full((1, 1), var + 1e-05, F32))
    diff = err - pltpu.roll(err, 127, 1)
    coef = jnp.concatenate([diff[:, i : i + 1] for i in (0, 2, 4, 6)], 0) / (spread * math.sqrt(64))
    key_ref[...] = outer(lk_ref[...].astype(F32) * coef, rk_ref[...])
    value_ref[...] = outer(lv_ref[...].astype(F32) * coef, rv_ref[...])


def update(err, left_key, right_key, left_value, right_value):
    args = [err, left_key, right_key, left_value, right_value]
    return call(
        update_kernel,
        "update",
        args,
        [whole(v.shape) for v in args],
        [array((128, 1024), F32), array((1024, 128), F32)],
        [whole((128, 1024)), whole((1024, 128))],
    )


def per_device(
    inputs,
    mix_key,
    key_weight,
    value_weight,
    key_left,
    key_right,
    value_left,
    value_right,
    pair_sign,
    targets,
):
    pop, mp = lax.axis_index("pop"), lax.axis_index("mp")
    x, zh, c = pop // 8, (pop // 2) % 4, pop % 2
    y, zl = mp // 2, mp % 2
    i32 = lambda *v: jnp.stack([jnp.asarray(e, jnp.int32) for e in v])

    def swap(values):
        return [move(v, c=1) for v in values]

    own_x, key_z = ring(key_weight, "x"), ring(key_weight, "zh")
    moved = transpose_xy(value_weight)
    rest = join([key_z[1], key_z[3], key_z[2]], [own_x[2], own_x[3], moved])
    mine, its, probe = mix(i32(c), inputs, mix_key, key_left, [rest])
    rest = [rest, step(rest, "x"), None, step(rest, "x", -1)]
    value_z = [moved, step(moved, "zh"), None, step(moved, "zh", -1)]
    rest[1], value_z[1] = fence([rest[1], value_z[1]], [rest[3], value_z[3]])
    rest[2], value_z[2] = step(rest[1], "x"), step(value_z[1], "zh")
    me = i32(x, zh, c)
    got = move(its, c=1)
    acc, other = both_step(me, mine, got, own_x, [rest[0], rest[1], rest[3]])
    (other,) = fence([other], [value_z[2]])
    slots = [(zh + (2 * c - 1) * k) % 4 for k in range(4)]
    slots = i32(*[jnp.where(s // 2 == zl, 2, 0) + s % 2 for s in slots])
    value_x = order(slots, value_z)
    got = move(other, c=1)
    vecs = [key_right.astype(F32), value_left.astype(F32)]
    base = last_step(me, mine, its, acc, got, *vecs, [rest[2], move(rest[2], c=1)], [value_x])

    (value_x,) = fence([value_x], [base])
    value_x = [value_x, step(value_x, "x"), None, step(value_x, "x", -1)]
    value_w = [move(value_x[0], c=1)]
    near = [base, step(base, "y"), None, step(base, "y", -1)]

    def to_owner(v):
        return v.reshape(2, 32, 128).transpose(1, 0, 2)

    def to_all(v):
        return jnp.broadcast_to(v.reshape(1, 16, 128), (32, 16, 128))

    sign = pair_sign.astype(BF)[:, None]
    parcel = jnp.concatenate(
        [
            to_owner(key_left * sign),
            to_owner(value_right),
            to_all(key_right),
            to_all(value_left * sign),
        ],
        1,
    )
    (parcel,) = fence([parcel], [base])
    parcel = lax.all_to_all(parcel, "pop", split_axis=0, concat_axis=0, tiled=True)

    def unpack(lo, hi):
        v = parcel[:, lo:hi].reshape(16, 2, 2, (hi - lo) // 2 * 128)
        return v.transpose(1, 2, 0, 3).reshape(64, (hi - lo) // 2 * 128)

    left_key, right_value = unpack(0, 2), unpack(2, 4)
    right_key, left_value = unpack(4, 20), unpack(20, 36)
    right = value_right.astype(F32)
    send_right, keep_right = (
        lax.dynamic_slice_in_dim(right, (2 * y + half) * 512, 512, 1) for half in (1 - zl, zl)
    )
    at = [i32(x, c, y, pair_sign[p]) for p in range(2)]
    value_x[1], near[1] = fence(
        [value_x[1], near[1]], [value_x[3], near[3], parcel, send_right, keep_right, *at]
    )
    value_x[2], near[2] = step(value_x[1], "x"), step(near[1], "y")
    value_w = (value_x, value_w + swap(value_x[1:]))

    hidden, got = [], []
    for p in range(2):
        send, *hid = send_step(at[p], near, probe, p, send_right, *value_w)
        hidden.append((send, *hid))
        got.append(move(send, zl=1))
    sends, hids, sides = zip(*hidden)
    keep = keep_step(at[0], hids, sides, keep_right, *value_w, sends)
    done = finish(i32(c), 0, keep[0], got[0], targets)
    outputs, err = finish(i32(c), 1, keep[1], got[1], targets, done)

    err = err + move(err, c=1)
    err = jnp.broadcast_to(err[None], (128, 1, 128))
    groups = [[place(at["x"], at["zh"], core, at["y"], at["zl"]) for at in everywhere() if at["c"] == core] for core in range(2)]
    err = lax.all_to_all(
        err, AXES, split_axis=0, concat_axis=0, tiled=True, axis_index_groups=groups
    )
    key_update, value_update = update(
        err.reshape(16, 8, 128), left_key, right_key, left_value, right_value
    )
    return outputs, key_update, value_update


def solution(mesh):
    in_specs = (
        P("pop", None, None),
        P(),
        P("pop", "mp"),
        P("mp", "pop"),
        P("pop", None),
        P("pop", "mp"),
        P("pop", "mp"),
        P("pop", None),
        P("pop"),
        P("pop", None, "mp"),
    )
    out_specs = (P("pop", None, "mp"), P("pop", "mp"), P("mp", "pop"))
    return jax.shard_map(
        per_device, mesh=mesh, in_specs=in_specs, out_specs=out_specs, check_vma=False
    )
```

```python
import functools
import math

import jax
import jax.numpy as jnp
from jax import lax
from jax.experimental import pallas as pl
from jax.experimental.pallas import tpu as pltpu
from jax.sharding import PartitionSpec as P

FF = 8192
D = 4096
SEQ = 256
BF = jnp.bfloat16
F32 = jnp.float32
AXES = ("pop", "mp")
SIZES = dict(x=4, zh=4, c=2, y=4, zl=2)


def place(x, zh, c, y, zl):
    return ((x * 4 + zh) * 2 + c) * 8 + y * 2 + zl


def everywhere():
    for x in range(4):
        for zh in range(4):
            for c in range(2):
                for y in range(4):
                    for zl in range(2):
                        yield dict(x=x, zh=zh, c=c, y=y, zl=zl)


def move(value, **shift):
    pairs = []
    for at in everywhere():
        to = {k: (v + shift.get(k, 0)) % SIZES[k] for k, v in at.items()}
        pairs.append((place(**at), place(**to)))
    return lax.ppermute(value, AXES, pairs)


def step(value, axis, way=1):
    pairs = []
    for at in everywhere():
        to = {**at, axis: (at[axis] + way * (1 - 2 * at["c"])) % SIZES[axis]}
        pairs.append((place(**at), place(**to)))
    return lax.ppermute(value, AXES, pairs)


def ring(value, axis):
    back = step(value, axis)
    return [value, back, step(back, axis), step(value, axis, -1)]


def transpose_xy(value):
    pairs = []
    for at in everywhere():
        pairs.append((place(**at), place(**{**at, "x": at["y"], "y": at["x"]})))
    return lax.ppermute(value, AXES, pairs)


ANY = pl.BlockSpec(memory_space=pltpu.HBM)


def whole(shape):
    return pl.BlockSpec(shape, lambda *_: (0,) * len(shape))


def call(kernel, name, args, specs, outs, out_specs, *, grid=(1,), scalars=None, tokens=(), scratch=(), us=1):
    lead = 0 if scalars is None else 1

    def body(*refs):
        kernel(*refs[:lead], *refs[lead + len(tokens) :])

    return pl.pallas_call(
        body,
        grid_spec=pltpu.PrefetchScalarGridSpec(
            num_scalar_prefetch=lead,
            grid=grid,
            in_specs=[ANY] * len(tokens) + list(specs),
            out_specs=out_specs,
            scratch_shapes=list(scratch),
        ),
        out_shape=outs,
        compiler_params=pltpu.CompilerParams(vmem_limit_bytes=64 * 2**20),
        cost_estimate=pl.CostEstimate(flops=us * 2**30, bytes_accessed=2**20, transcendentals=0),
        name=name,
    )(*([scalars] if lead else []), *tokens, *args)


def array(shape, dtype):
    return jax.ShapeDtypeStruct(shape, dtype)


def fence(values, tokens=(), us=1):
    count = len(values)
    return pl.pallas_call(
        lambda *refs: None,
        in_specs=[ANY] * (count + len(tokens)),
        out_specs=[ANY] * count,
        out_shape=[array(v.shape, v.dtype) for v in values],
        input_output_aliases={i: i for i in range(count)},
        compiler_params=pltpu.CompilerParams(vmem_limit_bytes=64 * 2**20),
        cost_estimate=pl.CostEstimate(flops=us * 2**30, bytes_accessed=2**20, transcendentals=0),
        name="fence",
    )(*values, *tokens)


def mix_kernel(
    s_ref, x_ref, mix_ref, left_ref, mine_ref, its_ref, probe_ref, in_buf, out_buf, in_sems, out_sems
):
    def load(i):
        p, x = lax.div(i, 4), lax.rem(i, 4)
        return pltpu.make_async_copy(
            x_ref.at[p, :, pl.ds(pl.multiple_of(x * 1024, 1024), 1024)], in_buf.at[i], in_sems.at[i]
        )

    def save(i):
        p, x = lax.div(i, 4), lax.rem(i, 4)
        rows = pl.ds(pl.multiple_of(p * SEQ, SEQ), SEQ)
        return [
            pltpu.make_async_copy(
                out_buf.at[i, :, core], ref.at[:, x, rows], out_sems.at[i, half]
            )
            for half, (core, ref) in enumerate(((s_ref[0], mine_ref), (1 - s_ref[0], its_ref)))
        ]

    for i in range(8):
        load(i).start()
    probe_ref[...] = jnp.zeros_like(probe_ref)
    row = lax.broadcasted_iota(jnp.int32, (SEQ, 256), 0)

    def one(i, carry):
        load(i).wait()
        p, x = lax.div(i, 4), lax.rem(i, 4)
        probe = jnp.zeros((SEQ, 128), F32)
        for zh in range(4):
            here = pl.ds(pl.multiple_of(x * 1024 + zh * 256, 256), 256)
            cur = in_buf[i, :, zh * 256 : (zh + 1) * 256].astype(F32)
            shifted = jnp.where(row == 0, 0.0, pltpu.roll(cur, 1, 0))
            mixed = (cur + (shifted - cur) * mix_ref[0:1, here]).astype(BF)
            left = jnp.where(p == 0, left_ref[0:1, here], left_ref[1:2, here]).astype(F32)
            prod = mixed.astype(F32) * left
            probe = probe + prod[:, :128] + prod[:, 128:]
            out_buf[i, zh, 0] = mixed[:, :128]
            out_buf[i, zh, 1] = mixed[:, 128:]
        probe_ref[p] += probe
        for copy in save(i):
            copy.start()
        return carry

    lax.fori_loop(0, 8, one, 0)
    for i in range(8):
        for copy in save(i):
            copy.wait()


def mix(scalars, inputs, mix_key, key_left, tokens=()):
    return call(
        mix_kernel,
        "mix",
        [inputs, mix_key.reshape(1, D), key_left],
        [ANY, whole((1, D)), whole((2, D))],
        [array((4, 4, 2 * SEQ, 128), BF)] * 2 + [array((2, SEQ, 128), F32)],
        [ANY, ANY, whole((2, SEQ, 128))],
        scalars=scalars,
        tokens=tokens,
        scratch=[
            pltpu.VMEM((8, SEQ, 1024), BF),
            pltpu.VMEM((8, 4, 2, SEQ, 128), BF),
            pltpu.SemaphoreType.DMA((8,)),
            pltpu.SemaphoreType.DMA((8, 2)),
        ],
        us=16,
    )


def gather(pieces, places, buf_ref, sems):
    loads = [
        pltpu.make_async_copy(ref, buf_ref.at[i], sems.at[i, 0]) for i, ref in enumerate(pieces)
    ]
    saves = [
        pltpu.make_async_copy(buf_ref.at[i], ref, sems.at[i, 1]) for i, ref in enumerate(places)
    ]
    for load in loads:
        load.start()
    for load, save in zip(loads, saves):
        load.wait()
        save.start()
    for save in saves:
        save.wait()


def join_kernel(*refs):
    out_ref, buf_ref, sems = refs[-3:]
    places = [out_ref.at[i * 128 : (i + 1) * 128] for i in range(3)]
    gather(refs[:3], places, buf_ref, sems)


def join(blocks, tokens):
    return call(
        join_kernel,
        "join",
        blocks,
        [ANY] * 3,
        array((384, 1024), BF),
        ANY,
        tokens=tokens,
        scratch=[pltpu.VMEM((3, 128, 1024), BF), pltpu.SemaphoreType.DMA((3, 2))],
        us=4,
    )


BACK = (1, 3, 2)


def both_kernel(s_ref, mine_ref, got_ref, *refs):
    own, rest, refs = refs[:4], refs[4:7], refs[7:]
    own_ref, other_ref, w_ref, in_ref, own_buf, other_buf, sems = refs
    x, zh, way = s_ref[0], s_ref[1], 2 * s_ref[2] - 1
    places = [(0, k) for k in range(4)] + [(back, k) for k in (0, 1, 3) for back in BACK]

    def rows(half, ref):
        copies = []
        for i, (back, k) in enumerate(places):
            at = lax.rem(zh + way * back + 4, 4)
            col = lax.rem(x + way * k + 4, 4)
            copies.append(
                pltpu.make_async_copy(
                    ref.at[at, col],
                    in_ref.at[half, :, i * 128 : i * 128 + 128],
                    sems.at[i, half],
                )
            )
        return copies

    weights = [
        pltpu.make_async_copy(own[k], w_ref.at[k * 128 : k * 128 + 128], sems.at[k, 2])
        for k in range(4)
    ]
    for k in range(3):
        row = 512 + k * 384
        weights.append(
            pltpu.make_async_copy(rest[k], w_ref.at[row : row + 384], sems.at[4 + k, 2])
        )
    first, second = rows(1, got_ref), rows(0, mine_ref)
    for copy in weights + first + second:
        copy.start()
    for copy in weights + first:
        copy.wait()
    other_buf[...] = jnp.dot(in_ref[1], w_ref[...], preferred_element_type=F32).astype(BF)
    save = pltpu.make_async_copy(other_buf, other_ref, sems.at[7, 2])
    save.start()
    for copy in second:
        copy.wait()
    saves = [save]
    for n in range(2):
        cols = slice(n * 512, n * 512 + 512)
        own_buf[n] = jnp.dot(in_ref[0], w_ref[:, cols], preferred_element_type=F32)
        save = pltpu.make_async_copy(own_buf.at[n], own_ref.at[n], sems.at[8 + n, 2])
        save.start()
        saves.append(save)
    for save in saves:
        save.wait()


def both_step(scalars, mine, got, own, rest, tokens=()):
    return call(
        both_kernel,
        "both",
        [mine, got, *own, *rest],
        [ANY] * 9,
        [array((2, 2 * SEQ, 512), F32), array((2 * SEQ, 1024), BF)],
        [ANY] * 2,
        scalars=scalars,
        tokens=tokens,
        scratch=[
            pltpu.VMEM((1664, 1024), BF),
            pltpu.VMEM((2, 512, 1664), BF),
            pltpu.VMEM((2, 512, 512), F32),
            pltpu.VMEM((512, 1024), BF),
            pltpu.SemaphoreType.DMA((13, 3)),
        ],
        us=24,
    )


def last_kernel(s_ref, mine_ref, its_ref, acc_ref, got_ref, right_ref, left_ref, *refs):
    blocks, (out_ref, w_ref, in_ref, acc_buf, got_buf, out_buf, sems) = refs[:2], refs[2:]
    x, zh, way = s_ref[0], s_ref[1], 2 * s_ref[2] - 1
    far = lax.rem(x + 2, 4)
    copies = []
    for half, (sign, ref) in enumerate(((way, mine_ref), (-way, its_ref))):
        row = half * 384
        copies.append(
            pltpu.make_async_copy(blocks[half], w_ref.at[row : row + 384], sems.at[half, 3])
        )
        for i, back in enumerate(BACK):
            at = lax.rem(zh + sign * back + 4, 4)
            col = row + i * 128
            copies.append(
                pltpu.make_async_copy(
                    ref.at[at, far], in_ref.at[:, col : col + 128], sems.at[half, i]
                )
            )
    sums = [
        pltpu.make_async_copy(got_ref, got_buf, sems.at[0, 4]),
        pltpu.make_async_copy(acc_ref, acc_buf, sems.at[1, 4]),
    ]
    for copy in copies + sums:
        copy.start()
    for copy in copies:
        copy.wait()
    right, left = right_ref[...].astype(F32), left_ref[...].astype(F32)
    row = lax.broadcasted_iota(jnp.int32, (16, 1024), 0)
    saves = []
    for p in range(2):
        rows = slice(p * SEQ, (p + 1) * SEQ)
        total = jnp.dot(in_ref[rows], w_ref[...], preferred_element_type=F32)
        if p == 0:
            for copy in sums:
                copy.wait()
        total = total + got_buf[rows].astype(F32)
        for n in range(2):
            cols = slice(n * 512, n * 512 + 512)
            out_buf[p, :SEQ, cols] = (total[:, cols] + acc_buf[n, rows]).astype(BF)
        tail = jnp.where(row == 1, left[p : p + 1], 0.0)
        out_buf[p, SEQ:] = jnp.where(row == 0, right[p : p + 1], tail).astype(BF)
        save = pltpu.make_async_copy(out_buf.at[p], out_ref.at[p], sems.at[p, 5])
        save.start()
        saves.append(save)
    for save in saves:
        save.wait()


def last_step(scalars, mine, its, acc, got, right, left, blocks, tokens=()):
    return call(
        last_kernel,
        "last",
        [mine, its, acc, got, right, left, *blocks],
        [ANY] * 4 + [whole((2, 1024))] * 2 + [ANY] * 2,
        array((2, SEQ + 16, 1024), BF),
        ANY,
        scalars=scalars,
        tokens=tokens,
        scratch=[
            pltpu.VMEM((768, 1024), BF),
            pltpu.VMEM((512, 768), BF),
            pltpu.VMEM((2, 512, 512), F32),
            pltpu.VMEM((512, 1024), BF),
            pltpu.VMEM((2, SEQ + 16, 1024), BF),
            pltpu.SemaphoreType.DMA((2, 6)),
        ],
        us=16,
    )


def order_kernel(s_ref, *refs):
    out_ref, buf_ref, sems = refs[4:]
    gather(refs[:4], [out_ref.at[s_ref[k]] for k in range(4)], buf_ref, sems)


def order(scalars, pieces, tokens=()):
    return call(
        order_kernel,
        "order",
        pieces,
        [ANY] * 4,
        array((4, 1024, 128), BF),
        ANY,
        scalars=scalars,
        tokens=tokens,
        scratch=[pltpu.VMEM((4, 1024, 128), BF), pltpu.SemaphoreType.DMA((4, 2))],
        us=4,
    )


def value_copies(s_ref, own, other, first, w_ref, sems):
    x, c = s_ref[0], s_ref[1]
    copies = []
    for k in range(4):
        for half, blocks in enumerate((own, other)):
            core = c if half == 0 else 1 - c
            at = lax.rem(x + (2 * core - 1) * k + 4, 4)
            for n in range(2):
                col = pl.multiple_of(core * 128 + n * 256, 128)
                copy = pltpu.make_async_copy(
                    blocks[k].at[first + n],
                    w_ref.at[at, :, pl.ds(col, 128)],
                    sems.at[k, half, n],
                )
                copy.start()
                copies.append(copy)
    return copies


def add_side(total, side_ref, right_ref, out_ref):
    for n in range(4):
        cols = slice(n * 128, (n + 1) * 128)
        out = total[:, cols] + side_ref[...] * right_ref[:, cols]
        out_ref[:, cols] = out.astype(out_ref.dtype)


def send_kernel(pair, s_ref, b0, b1, b2, b3, probe_ref, right_ref, *refs):
    own, other, refs = refs[:4], refs[4:8], refs[8:]
    out_ref, h_out, side_ref, b_ref, h_ref, w_ref, h_sems, sems = refs
    loads = [
        pltpu.make_async_copy(base.at[pair], b_ref.at[k], h_sems.at[4 + k])
        for k, base in enumerate((b0, b1, b2, b3))
    ]
    loads[0].start()
    copies = value_copies(s_ref, own, other, 0, w_ref, sems)
    for load in loads[1:]:
        load.start()
    y, way, sign = s_ref[2], 2 * s_ref[1] - 1, s_ref[3].astype(F32)
    probe_all = jnp.sum(probe_ref[0], axis=1, keepdims=True) * (0.5 * sign / math.sqrt(D))
    side_ref[...] = jnp.zeros_like(side_ref)

    def hide(k):
        loads[k].wait()
        vecs = b_ref[k, SEQ:, :].astype(F32)
        for lo in range(0, SEQ, 128):
            rows = slice(lo, lo + 128)
            side = [jnp.zeros((128, 128), F32), jnp.zeros((128, 128), F32)]
            for col in range(0, 1024, 256):
                cols = slice(col, col + 256)
                act = b_ref[k, rows, cols].astype(F32)
                nudge = probe_all[rows] * vecs[0:1, cols]
                left = vecs[1:2, cols]
                for m, pre in enumerate((act + nudge, act - nudge)):
                    pre = jnp.maximum(pre, 0.0)
                    square = pre * pre
                    h_ref[k, m * SEQ + lo : m * SEQ + lo + 128, cols] = square.astype(BF)
                    prod = square * left
                    side[m] = side[m] + prod[:, :128] + prod[:, 128:]
            for m in range(2):
                side_ref[m * SEQ + lo : m * SEQ + lo + 128, :] += side[m]
        save = pltpu.make_async_copy(h_ref.at[k], h_out.at[k], h_sems.at[k])
        save.start()
        return save

    saves = [hide(k) for k in range(4)]
    for copy in copies:
        copy.wait()
    total = None
    for k in range(4):
        at = lax.rem(y + way * k + 4, 4)
        part = jnp.dot(h_ref[k], w_ref[at], preferred_element_type=F32)
        total = part if total is None else total + part
    scale = 0.5 / math.sqrt(FF) * sign
    for m in range(2):
        rows = slice(m * SEQ, (m + 1) * SEQ)
        side = jnp.sum(side_ref[rows, :], axis=1, keepdims=True) * (scale if m == 0 else -scale)
        side_ref[rows, :] = jnp.broadcast_to(side, (SEQ, 128))
    add_side(total, side_ref, right_ref.at[pair : pair + 1], out_ref)
    for save in saves:
        save.wait()


def send_step(scalars, base, probe, pair, right, own, other, tokens=()):
    return call(
        functools.partial(send_kernel, pair),
        "send",
        [*base, probe, right, *own, *other],
        [ANY] * 4
        + [pl.BlockSpec((1, SEQ, 128), lambda i, s: (pair, 0, 0)), whole((2, 512))]
        + [ANY] * 8,
        [
            array((2 * SEQ, 512), BF),
            array((4, 2 * SEQ, 1024), BF),
            array((2 * SEQ, 128), F32),
        ],
        [whole((2 * SEQ, 512)), ANY, whole((2 * SEQ, 128))],
        scalars=scalars,
        tokens=tokens,
        scratch=[
            pltpu.VMEM((4, SEQ + 16, 1024), BF),
            pltpu.VMEM((4, 2 * SEQ, 1024), BF),
            pltpu.VMEM((4, 1024, 512), BF),
            pltpu.SemaphoreType.DMA((8,)),
            pltpu.SemaphoreType.DMA((4, 2, 2)),
        ],
        us=16,
    )


def keep_kernel(s_ref, h0, h1, side0, side1, right_ref, *refs):
    own, other, refs = refs[:4], refs[4:8], refs[8:]
    out0, out1, h_ref, w_ref, out_buf, h_sems, sems = refs
    loads = [
        [pltpu.make_async_copy(h.at[k], h_ref.at[p, k], h_sems.at[p, k]) for k in range(4)]
        for p, h in enumerate((h0, h1))
    ]
    loads[0][0].start()
    copies = value_copies(s_ref, own, other, 2, w_ref, sems)
    for load in loads[0][1:] + loads[1]:
        load.start()
    y, way = s_ref[2], 2 * s_ref[1] - 1
    for copy in copies:
        copy.wait()
    saves = []
    for p, (side_ref, out_ref) in enumerate(((side0, out0), (side1, out1))):
        total = None
        for k in range(4):
            loads[p][k].wait()
            at = lax.rem(y + way * k + 4, 4)
            part = jnp.dot(h_ref[p, k], w_ref[at], preferred_element_type=F32)
            total = part if total is None else total + part
        add_side(total, side_ref, right_ref.at[p : p + 1], out_buf.at[p])
        save = pltpu.make_async_copy(out_buf.at[p], out_ref, h_sems.at[p, 4])
        save.start()
        saves.append(save)
    for save in saves:
        save.wait()


def keep_step(scalars, hidden, side, right, own, other, tokens=()):
    return call(
        keep_kernel,
        "keep",
        [*hidden, *side, right, *own, *other],
        [ANY] * 2 + [whole((2 * SEQ, 128))] * 2 + [whole((2, 512))] + [ANY] * 8,
        [array((2 * SEQ, 512), F32)] * 2,
        [ANY] * 2,
        scalars=scalars,
        tokens=tokens,
        scratch=[
            pltpu.VMEM((2, 4, 2 * SEQ, 1024), BF),
            pltpu.VMEM((4, 1024, 512), BF),
            pltpu.VMEM((2, 2 * SEQ, 512), F32),
            pltpu.SemaphoreType.DMA((2, 5)),
            pltpu.SemaphoreType.DMA((4, 2, 2)),
        ],
        us=16,
    )


def finish_kernel(pair, s_ref, *refs):
    errs = jnp.zeros((1, 128), F32)
    if pair == 1:
        errs = refs[1][...]
        refs = refs[2:]
    keep_ref, got_ref, target_ref, out_ref, err_ref = refs
    target = target_ref[0].astype(F32)
    lane = lax.broadcasted_iota(jnp.int32, (1, 128), 1)
    for m in range(2):
        rows = slice(m * SEQ, (m + 1) * SEQ)
        out = (keep_ref[rows, :] + got_ref[rows, :].astype(F32)).astype(BF)
        out_ref[m] = out
        gap = out.astype(F32) - target
        err = jnp.sum(gap * gap)
        errs = errs + jnp.where(lane == 4 * s_ref[0] + 2 * pair + m, err, 0.0)
    err_ref[...] = errs


def finish(scalars, pair, keep, got, targets, done=()):
    return pl.pallas_call(
        functools.partial(finish_kernel, pair),
        grid_spec=pltpu.PrefetchScalarGridSpec(
            num_scalar_prefetch=1,
            grid=(1,),
            in_specs=([ANY, whole((1, 128))] if done else [])
            + [whole((2 * SEQ, 512))] * 2
            + [pl.BlockSpec((1, SEQ, 512), lambda i, s: (pair, 0, 0))],
            out_specs=[pl.BlockSpec((2, SEQ, 512), lambda i, s: (pair, 0, 0)), whole((1, 128))],
        ),
        out_shape=[array((4, SEQ, 512), BF), array((1, 128), F32)],
        input_output_aliases={1: 0} if done else {},
        compiler_params=pltpu.CompilerParams(vmem_limit_bytes=64 * 2**20),
        cost_estimate=pl.CostEstimate(flops=2**31, bytes_accessed=2**20, transcendentals=0),
        name="finish",
    )(scalars, *done, keep, got, targets)


def outer(left, right):
    high = left.astype(BF)
    low = (left - high.astype(F32)).astype(BF)
    left = jnp.concatenate([high, low], 0)
    right = jnp.concatenate([right, right], 0)
    return lax.dot_general(left, right, (((0,), (0,)), ((), ())), preferred_element_type=F32)


def update_kernel(err_ref, lk_ref, rk_ref, lv_ref, rv_ref, key_ref, value_ref):
    err = jnp.sum(err_ref[...], axis=1) / (SEQ * D)
    lane = lax.broadcasted_iota(jnp.int32, err.shape, 1)
    used = lane < 8
    mean = jnp.sum(jnp.where(used, err, 0.0)) / 128
    var = jnp.sum(jnp.where(used, (err - mean) * (err - mean), 0.0)) / 128
    spread = jnp.sqrt(jnp.full((1, 1), var + 1e-05, F32))
    diff = err - pltpu.roll(err, 127, 1)
    coef = jnp.concatenate([diff[:, i : i + 1] for i in (0, 2, 4, 6)], 0) / (spread * math.sqrt(64))
    key_ref[...] = outer(lk_ref[...].astype(F32) * coef, rk_ref[...])
    value_ref[...] = outer(lv_ref[...].astype(F32) * coef, rv_ref[...])


def update(err, left_key, right_key, left_value, right_value):
    args = [err, left_key, right_key, left_value, right_value]
    return call(
        update_kernel,
        "update",
        args,
        [whole(v.shape) for v in args],
        [array((128, 1024), F32), array((1024, 128), F32)],
        [whole((128, 1024)), whole((1024, 128))],
    )


def per_device(
    inputs,
    mix_key,
    key_weight,
    value_weight,
    key_left,
    key_right,
    value_left,
    value_right,
    pair_sign,
    targets,
):
    pop, mp = lax.axis_index("pop"), lax.axis_index("mp")
    x, zh, c = pop // 8, (pop // 2) % 4, pop % 2
    y, zl = mp // 2, mp % 2
    i32 = lambda *v: jnp.stack([jnp.asarray(e, jnp.int32) for e in v])

    def swap(values):
        return [move(v, c=1) for v in values]

    own_x, key_z = ring(key_weight, "x"), ring(key_weight, "zh")
    moved = transpose_xy(value_weight)
    rest = join([key_z[1], key_z[3], key_z[2]], [own_x[2], own_x[3], moved])
    mine, its, probe = mix(i32(c), inputs, mix_key, key_left, [rest])
    rest = [rest, step(rest, "x"), None, step(rest, "x", -1)]
    value_z = [moved, step(moved, "zh"), None, step(moved, "zh", -1)]
    rest[1], value_z[1] = fence([rest[1], value_z[1]], [rest[3]], us=24)
    rest[2], value_z[2] = step(rest[1], "x"), step(value_z[1], "zh")
    me = i32(x, zh, c)
    got = move(its, c=1)
    acc, other = both_step(me, mine, got, own_x, [rest[0], rest[1], rest[3]])
    slots = [(zh + (2 * c - 1) * k) % 4 for k in range(4)]
    slots = i32(*[jnp.where(s // 2 == zl, 2, 0) + s % 2 for s in slots])
    value_x = order(slots, value_z)
    (other,) = fence([other], [value_z[2], value_z[3]])
    got = move(other, c=1)
    vecs = [key_right, value_left]
    base = last_step(me, mine, its, acc, got, *vecs, [rest[2], move(rest[2], c=1)], [value_x])

    (value_x,) = fence([value_x], [base])
    value_x = [value_x, step(value_x, "x"), None, step(value_x, "x", -1)]
    value_w = [move(value_x[0], c=1)]
    near = [base, step(base, "y"), None, step(base, "y", -1)]

    def to_owner(v):
        return v.reshape(2, 32, 128).transpose(1, 0, 2)

    def to_all(v):
        return jnp.broadcast_to(v.reshape(1, 16, 128), (32, 16, 128))

    (sign,) = fence([pair_sign], [base])
    sign = sign.astype(BF)[:, None]
    parcel = jnp.concatenate(
        [
            to_owner(key_left * sign),
            to_owner(value_right),
            to_all(key_right),
            to_all(value_left * sign),
        ],
        1,
    )
    (parcel,) = fence([parcel], [base])
    parcel = lax.all_to_all(parcel, "pop", split_axis=0, concat_axis=0, tiled=True)

    def unpack(lo, hi):
        v = parcel[:, lo:hi].reshape(16, 2, 2, (hi - lo) // 2 * 128)
        return v.transpose(1, 2, 0, 3).reshape(64, (hi - lo) // 2 * 128)

    left_key, right_value = unpack(0, 2), unpack(2, 4)
    right_key, left_value = unpack(4, 20), unpack(20, 36)
    right = value_right.astype(F32)
    send_right, keep_right = (
        lax.dynamic_slice_in_dim(right, (2 * y + half) * 512, 512, 1) for half in (1 - zl, zl)
    )
    at = [i32(x, c, y, pair_sign[p]) for p in range(2)]
    value_x[1], near[1] = fence(
        [value_x[1], near[1]], [value_x[3], near[3], parcel, send_right, keep_right, *at]
    )
    value_x[2], near[2] = step(value_x[1], "x"), step(near[1], "y")
    value_w = (value_x, value_w + swap(value_x[1:]))

    hidden, got = [], []
    for p in range(2):
        send, *hid = send_step(at[p], near, probe, p, send_right, *value_w)
        hidden.append((send, *hid))
        got.append(move(send, zl=1))
    sends, hids, sides = zip(*hidden)
    keep = keep_step(at[0], hids, sides, keep_right, *value_w, sends)
    done = finish(i32(c), 0, keep[0], got[0], targets)
    outputs, err = finish(i32(c), 1, keep[1], got[1], targets, done)

    err = err + move(err, c=1)
    err = jnp.broadcast_to(err[None], (128, 1, 128))
    groups = [[place(at["x"], at["zh"], core, at["y"], at["zl"]) for at in everywhere() if at["c"] == core] for core in range(2)]
    err = lax.all_to_all(
        err, AXES, split_axis=0, concat_axis=0, tiled=True, axis_index_groups=groups
    )
    key_update, value_update = update(
        err.reshape(16, 8, 128), left_key, right_key, left_value, right_value
    )
    return outputs, key_update, value_update


def solution(mesh):
    in_specs = (
        P("pop", None, None),
        P(),
        P("pop", "mp"),
        P("mp", "pop"),
        P("pop", None),
        P("pop", "mp"),
        P("pop", "mp"),
        P("pop", None),
        P("pop"),
        P("pop", None, "mp"),
    )
    out_specs = (P("pop", None, "mp"), P("pop", "mp"), P("mp", "pop"))
    return jax.shard_map(
        per_device, mesh=mesh, in_specs=in_specs, out_specs=out_specs, check_vma=False
    )
```

```python
import functools
import math

import jax
import jax.numpy as jnp
from jax import lax
from jax.experimental import pallas as pl
from jax.experimental.pallas import tpu as pltpu
from jax.sharding import PartitionSpec as P

FF = 8192
D = 4096
SEQ = 256
BF = jnp.bfloat16
F32 = jnp.float32
AXES = ("pop", "mp")
SIZES = dict(x=4, zh=4, c=2, y=4, zl=2)


def place(x, zh, c, y, zl):
    return ((x * 4 + zh) * 2 + c) * 8 + y * 2 + zl


def everywhere():
    for x in range(4):
        for zh in range(4):
            for c in range(2):
                for y in range(4):
                    for zl in range(2):
                        yield dict(x=x, zh=zh, c=c, y=y, zl=zl)


def move(value, **shift):
    pairs = []
    for at in everywhere():
        to = {k: (v + shift.get(k, 0)) % SIZES[k] for k, v in at.items()}
        pairs.append((place(**at), place(**to)))
    return lax.ppermute(value, AXES, pairs)


def step(value, axis, way=1):
    pairs = []
    for at in everywhere():
        to = {**at, axis: (at[axis] + way * (1 - 2 * at["c"])) % SIZES[axis]}
        pairs.append((place(**at), place(**to)))
    return lax.ppermute(value, AXES, pairs)


def ring(value, axis):
    back = step(value, axis)
    return [value, back, step(back, axis), step(value, axis, -1)]


def transpose_xy(value):
    pairs = []
    for at in everywhere():
        pairs.append((place(**at), place(**{**at, "x": at["y"], "y": at["x"]})))
    return lax.ppermute(value, AXES, pairs)


ANY = pl.BlockSpec(memory_space=pltpu.HBM)


def whole(shape):
    return pl.BlockSpec(shape, lambda *_: (0,) * len(shape))


def call(kernel, name, args, specs, outs, out_specs, *, grid=(1,), scalars=None, tokens=(), scratch=(), us=1):
    lead = 0 if scalars is None else 1

    def body(*refs):
        kernel(*refs[:lead], *refs[lead + len(tokens) :])

    return pl.pallas_call(
        body,
        grid_spec=pltpu.PrefetchScalarGridSpec(
            num_scalar_prefetch=lead,
            grid=grid,
            in_specs=[ANY] * len(tokens) + list(specs),
            out_specs=out_specs,
            scratch_shapes=list(scratch),
        ),
        out_shape=outs,
        compiler_params=pltpu.CompilerParams(vmem_limit_bytes=64 * 2**20),
        cost_estimate=pl.CostEstimate(flops=us * 2**30, bytes_accessed=2**20, transcendentals=0),
        name=name,
    )(*([scalars] if lead else []), *tokens, *args)


def array(shape, dtype):
    return jax.ShapeDtypeStruct(shape, dtype)


def fence(values, tokens=(), us=1):
    count = len(values)
    return pl.pallas_call(
        lambda *refs: None,
        in_specs=[ANY] * (count + len(tokens)),
        out_specs=[ANY] * count,
        out_shape=[array(v.shape, v.dtype) for v in values],
        input_output_aliases={i: i for i in range(count)},
        compiler_params=pltpu.CompilerParams(vmem_limit_bytes=64 * 2**20),
        cost_estimate=pl.CostEstimate(flops=us * 2**30, bytes_accessed=2**20, transcendentals=0),
        name="fence",
    )(*values, *tokens)


def mix_kernel(
    s_ref, x_ref, mix_ref, left_ref, mine_ref, its_ref, probe_ref, in_buf, out_buf, in_sems, out_sems
):
    def load(i):
        p, x = lax.div(i, 4), lax.rem(i, 4)
        return pltpu.make_async_copy(
            x_ref.at[p, :, pl.ds(pl.multiple_of(x * 1024, 1024), 1024)], in_buf.at[i], in_sems.at[i]
        )

    def save(i):
        p, x = lax.div(i, 4), lax.rem(i, 4)
        rows = pl.ds(pl.multiple_of(p * SEQ, SEQ), SEQ)
        return [
            pltpu.make_async_copy(
                out_buf.at[i, :, core], ref.at[:, x, rows], out_sems.at[i, half]
            )
            for half, (core, ref) in enumerate(((s_ref[0], mine_ref), (1 - s_ref[0], its_ref)))
        ]

    for i in range(8):
        load(i).start()
    probe_ref[...] = jnp.zeros_like(probe_ref)
    row = lax.broadcasted_iota(jnp.int32, (SEQ, 256), 0)

    def one(i, carry):
        load(i).wait()
        p, x = lax.div(i, 4), lax.rem(i, 4)
        probe = jnp.zeros((SEQ, 128), F32)
        for zh in range(4):
            here = pl.ds(pl.multiple_of(x * 1024 + zh * 256, 256), 256)
            cur = in_buf[i, :, zh * 256 : (zh + 1) * 256].astype(F32)
            shifted = jnp.where(row == 0, 0.0, pltpu.roll(cur, 1, 0))
            mixed = (cur + (shifted - cur) * mix_ref[0:1, here]).astype(BF)
            left = jnp.where(p == 0, left_ref[0:1, here], left_ref[1:2, here]).astype(F32)
            prod = mixed.astype(F32) * left
            probe = probe + prod[:, :128] + prod[:, 128:]
            out_buf[i, zh, 0] = mixed[:, :128]
            out_buf[i, zh, 1] = mixed[:, 128:]
        probe_ref[p] += probe
        for copy in save(i):
            copy.start()
        return carry

    lax.fori_loop(0, 8, one, 0)
    for i in range(8):
        for copy in save(i):
            copy.wait()


def mix(scalars, inputs, mix_key, key_left, tokens=()):
    return call(
        mix_kernel,
        "mix",
        [inputs, mix_key.reshape(1, D), key_left],
        [ANY, whole((1, D)), whole((2, D))],
        [array((4, 4, 2 * SEQ, 128), BF)] * 2 + [array((2, SEQ, 128), F32)],
        [ANY, ANY, whole((2, SEQ, 128))],
        scalars=scalars,
        tokens=tokens,
        scratch=[
            pltpu.VMEM((8, SEQ, 1024), BF),
            pltpu.VMEM((8, 4, 2, SEQ, 128), BF),
            pltpu.SemaphoreType.DMA((8,)),
            pltpu.SemaphoreType.DMA((8, 2)),
        ],
        us=16,
    )


def gather(pieces, places, buf_ref, sems):
    loads = [
        pltpu.make_async_copy(ref, buf_ref.at[i], sems.at[i, 0]) for i, ref in enumerate(pieces)
    ]
    saves = [
        pltpu.make_async_copy(buf_ref.at[i], ref, sems.at[i, 1]) for i, ref in enumerate(places)
    ]
    for load in loads:
        load.start()
    for load, save in zip(loads, saves):
        load.wait()
        save.start()
    for save in saves:
        save.wait()


def join_kernel(*refs):
    out_ref, buf_ref, sems = refs[-3:]
    places = [out_ref.at[i * 128 : (i + 1) * 128] for i in range(3)]
    gather(refs[:3], places, buf_ref, sems)


def join(blocks, tokens):
    return call(
        join_kernel,
        "join",
        blocks,
        [ANY] * 3,
        array((384, 1024), BF),
        ANY,
        tokens=tokens,
        scratch=[pltpu.VMEM((3, 128, 1024), BF), pltpu.SemaphoreType.DMA((3, 2))],
        us=4,
    )


BACK = (1, 3, 2)


def both_kernel(s_ref, mine_ref, got_ref, *refs):
    own, rest, refs = refs[:4], refs[4:7], refs[7:]
    own_ref, other_ref, w_ref, in_ref, own_buf, other_buf, sems = refs
    x, zh, way = s_ref[0], s_ref[1], 2 * s_ref[2] - 1
    places = [(0, k) for k in range(4)] + [(back, k) for k in (0, 1, 3) for back in BACK]

    def rows(half, ref):
        copies = []
        for i, (back, k) in enumerate(places):
            at = lax.rem(zh + way * back + 4, 4)
            col = lax.rem(x + way * k + 4, 4)
            copies.append(
                pltpu.make_async_copy(
                    ref.at[at, col],
                    in_ref.at[half, :, i * 128 : i * 128 + 128],
                    sems.at[i, half],
                )
            )
        return copies

    weights = [
        pltpu.make_async_copy(own[k], w_ref.at[k * 128 : k * 128 + 128], sems.at[k, 2])
        for k in range(4)
    ]
    for k in range(3):
        row = 512 + k * 384
        weights.append(
            pltpu.make_async_copy(rest[k], w_ref.at[row : row + 384], sems.at[4 + k, 2])
        )
    first, second = rows(1, got_ref), rows(0, mine_ref)
    for copy in weights + first + second:
        copy.start()
    for copy in weights + first:
        copy.wait()
    other_buf[...] = jnp.dot(in_ref[1], w_ref[...], preferred_element_type=F32).astype(BF)
    save = pltpu.make_async_copy(other_buf, other_ref, sems.at[7, 2])
    save.start()
    for copy in second:
        copy.wait()
    saves = [save]
    for n in range(2):
        cols = slice(n * 512, n * 512 + 512)
        own_buf[n] = jnp.dot(in_ref[0], w_ref[:, cols], preferred_element_type=F32)
        save = pltpu.make_async_copy(own_buf.at[n], own_ref.at[n], sems.at[8 + n, 2])
        save.start()
        saves.append(save)
    for save in saves:
        save.wait()


def both_step(scalars, mine, got, own, rest, tokens=()):
    return call(
        both_kernel,
        "both",
        [mine, got, *own, *rest],
        [ANY] * 9,
        [array((2, 2 * SEQ, 512), F32), array((2 * SEQ, 1024), BF)],
        [ANY] * 2,
        scalars=scalars,
        tokens=tokens,
        scratch=[
            pltpu.VMEM((1664, 1024), BF),
            pltpu.VMEM((2, 512, 1664), BF),
            pltpu.VMEM((2, 512, 512), F32),
            pltpu.VMEM((512, 1024), BF),
            pltpu.SemaphoreType.DMA((13, 3)),
        ],
        us=24,
    )


def last_kernel(s_ref, mine_ref, its_ref, acc_ref, got_ref, right_ref, left_ref, *refs):
    blocks, (out_ref, w_ref, in_ref, acc_buf, got_buf, out_buf, sems) = refs[:2], refs[2:]
    x, zh, way = s_ref[0], s_ref[1], 2 * s_ref[2] - 1
    far = lax.rem(x + 2, 4)
    copies = []
    for half, (sign, ref) in enumerate(((way, mine_ref), (-way, its_ref))):
        row = half * 384
        copies.append(
            pltpu.make_async_copy(blocks[half], w_ref.at[row : row + 384], sems.at[half, 3])
        )
        for i, back in enumerate(BACK):
            at = lax.rem(zh + sign * back + 4, 4)
            col = row + i * 128
            copies.append(
                pltpu.make_async_copy(
                    ref.at[at, far], in_ref.at[:, col : col + 128], sems.at[half, i]
                )
            )
    sums = [
        pltpu.make_async_copy(got_ref, got_buf, sems.at[0, 4]),
        pltpu.make_async_copy(acc_ref, acc_buf, sems.at[1, 4]),
    ]
    for copy in copies + sums:
        copy.start()
    for copy in copies:
        copy.wait()
    right, left = right_ref[...].astype(F32), left_ref[...].astype(F32)
    row = lax.broadcasted_iota(jnp.int32, (16, 1024), 0)
    saves = []
    for p in range(2):
        rows = slice(p * SEQ, (p + 1) * SEQ)
        total = jnp.dot(in_ref[rows], w_ref[...], preferred_element_type=F32)
        if p == 0:
            for copy in sums:
                copy.wait()
        total = total + got_buf[rows].astype(F32)
        for n in range(2):
            cols = slice(n * 512, n * 512 + 512)
            out_buf[p, :SEQ, cols] = (total[:, cols] + acc_buf[n, rows]).astype(BF)
        tail = jnp.where(row == 1, left[p : p + 1], 0.0)
        out_buf[p, SEQ:] = jnp.where(row == 0, right[p : p + 1], tail).astype(BF)
        save = pltpu.make_async_copy(out_buf.at[p], out_ref.at[p], sems.at[p, 5])
        save.start()
        saves.append(save)
    for save in saves:
        save.wait()


def last_step(scalars, mine, its, acc, got, right, left, blocks, tokens=()):
    return call(
        last_kernel,
        "last",
        [mine, its, acc, got, right, left, *blocks],
        [ANY] * 4 + [whole((2, 1024))] * 2 + [ANY] * 2,
        array((2, SEQ + 16, 1024), BF),
        ANY,
        scalars=scalars,
        tokens=tokens,
        scratch=[
            pltpu.VMEM((768, 1024), BF),
            pltpu.VMEM((512, 768), BF),
            pltpu.VMEM((2, 512, 512), F32),
            pltpu.VMEM((512, 1024), BF),
            pltpu.VMEM((2, SEQ + 16, 1024), BF),
            pltpu.SemaphoreType.DMA((2, 6)),
        ],
        us=16,
    )


def order_kernel(s_ref, *refs):
    out_ref, buf_ref, sems = refs[4:]
    gather(refs[:4], [out_ref.at[s_ref[k]] for k in range(4)], buf_ref, sems)


def order(scalars, pieces, tokens=()):
    return call(
        order_kernel,
        "order",
        pieces,
        [ANY] * 4,
        array((4, 1024, 128), BF),
        ANY,
        scalars=scalars,
        tokens=tokens,
        scratch=[pltpu.VMEM((4, 1024, 128), BF), pltpu.SemaphoreType.DMA((4, 2))],
        us=4,
    )


def value_copies(s_ref, own, other, first, w_ref, sems):
    x, c = s_ref[0], s_ref[1]
    copies = []
    for k in range(4):
        for half, blocks in enumerate((own, other)):
            core = c if half == 0 else 1 - c
            at = lax.rem(x + (2 * core - 1) * k + 4, 4)
            for n in range(2):
                col = pl.multiple_of(core * 128 + n * 256, 128)
                copy = pltpu.make_async_copy(
                    blocks[k].at[first + n],
                    w_ref.at[at, :, pl.ds(col, 128)],
                    sems.at[k, half, n],
                )
                copy.start()
                copies.append(copy)
    return copies


def add_side(total, side_ref, right_ref, out_ref):
    for n in range(4):
        cols = slice(n * 128, (n + 1) * 128)
        out = total[:, cols] + side_ref[...] * right_ref[:, cols]
        out_ref[:, cols] = out.astype(out_ref.dtype)


def send_kernel(pair, s_ref, b0, b1, b2, b3, probe_ref, right_ref, *refs):
    own, other, refs = refs[:4], refs[4:8], refs[8:]
    out_ref, h_out, side_ref, b_ref, h_ref, w_ref, h_sems, sems = refs
    loads = [
        pltpu.make_async_copy(base.at[pair], b_ref.at[k], h_sems.at[4 + k])
        for k, base in enumerate((b0, b1, b2, b3))
    ]
    loads[0].start()
    copies = value_copies(s_ref, own, other, 0, w_ref, sems)
    for load in loads[1:]:
        load.start()
    y, way, sign = s_ref[2], 2 * s_ref[1] - 1, s_ref[3].astype(F32)
    probe_all = jnp.sum(probe_ref[0], axis=1, keepdims=True) * (0.5 * sign / math.sqrt(D))
    side_ref[...] = jnp.zeros_like(side_ref)

    def hide(k):
        loads[k].wait()
        vecs = b_ref[k, SEQ:, :].astype(F32)
        for lo in range(0, SEQ, 128):
            rows = slice(lo, lo + 128)
            side = [jnp.zeros((128, 128), F32), jnp.zeros((128, 128), F32)]
            for col in range(0, 1024, 256):
                cols = slice(col, col + 256)
                act = b_ref[k, rows, cols].astype(F32)
                nudge = probe_all[rows] * vecs[0:1, cols]
                left = vecs[1:2, cols]
                for m, pre in enumerate((act + nudge, act - nudge)):
                    pre = jnp.maximum(pre, 0.0)
                    square = pre * pre
                    h_ref[k, m * SEQ + lo : m * SEQ + lo + 128, cols] = square.astype(BF)
                    prod = square * left
                    side[m] = side[m] + prod[:, :128] + prod[:, 128:]
            for m in range(2):
                side_ref[m * SEQ + lo : m * SEQ + lo + 128, :] += side[m]
        save = pltpu.make_async_copy(h_ref.at[k], h_out.at[k], h_sems.at[k])
        save.start()
        return save

    saves = [hide(k) for k in range(4)]
    for copy in copies:
        copy.wait()
    total = None
    for k in range(4):
        at = lax.rem(y + way * k + 4, 4)
        part = jnp.dot(h_ref[k], w_ref[at], preferred_element_type=F32)
        total = part if total is None else total + part
    scale = 0.5 / math.sqrt(FF) * sign
    for m in range(2):
        rows = slice(m * SEQ, (m + 1) * SEQ)
        side = jnp.sum(side_ref[rows, :], axis=1, keepdims=True) * (scale if m == 0 else -scale)
        side_ref[rows, :] = jnp.broadcast_to(side, (SEQ, 128))
    add_side(total, side_ref, right_ref.at[pair : pair + 1], out_ref)
    for save in saves:
        save.wait()


def send_step(scalars, base, probe, pair, right, own, other, tokens=()):
    return call(
        functools.partial(send_kernel, pair),
        "send",
        [*base, probe, right, *own, *other],
        [ANY] * 4
        + [pl.BlockSpec((1, SEQ, 128), lambda i, s: (pair, 0, 0)), whole((2, 512))]
        + [ANY] * 8,
        [
            array((2 * SEQ, 512), BF),
            array((4, 2 * SEQ, 1024), BF),
            array((2 * SEQ, 128), F32),
        ],
        [whole((2 * SEQ, 512)), ANY, whole((2 * SEQ, 128))],
        scalars=scalars,
        tokens=tokens,
        scratch=[
            pltpu.VMEM((4, SEQ + 16, 1024), BF),
            pltpu.VMEM((4, 2 * SEQ, 1024), BF),
            pltpu.VMEM((4, 1024, 512), BF),
            pltpu.SemaphoreType.DMA((8,)),
            pltpu.SemaphoreType.DMA((4, 2, 2)),
        ],
        us=16,
    )


def keep_kernel(s_ref, h0, h1, side0, side1, right_ref, *refs):
    own, other, refs = refs[:4], refs[4:8], refs[8:]
    out0, out1, h_ref, w_ref, out_buf, h_sems, sems = refs
    loads = [
        [pltpu.make_async_copy(h.at[k], h_ref.at[p, k], h_sems.at[p, k]) for k in range(4)]
        for p, h in enumerate((h0, h1))
    ]
    loads[0][0].start()
    copies = value_copies(s_ref, own, other, 2, w_ref, sems)
    for load in loads[0][1:] + loads[1]:
        load.start()
    y, way = s_ref[2], 2 * s_ref[1] - 1
    for copy in copies:
        copy.wait()
    saves = []
    for p, (side_ref, out_ref) in enumerate(((side0, out0), (side1, out1))):
        total = None
        for k in range(4):
            loads[p][k].wait()
            at = lax.rem(y + way * k + 4, 4)
            part = jnp.dot(h_ref[p, k], w_ref[at], preferred_element_type=F32)
            total = part if total is None else total + part
        add_side(total, side_ref, right_ref.at[p : p + 1], out_buf.at[p])
        save = pltpu.make_async_copy(out_buf.at[p], out_ref, h_sems.at[p, 4])
        save.start()
        saves.append(save)
    for save in saves:
        save.wait()


def keep_step(scalars, hidden, side, right, own, other, tokens=()):
    return call(
        keep_kernel,
        "keep",
        [*hidden, *side, right, *own, *other],
        [ANY] * 2 + [whole((2 * SEQ, 128))] * 2 + [whole((2, 512))] + [ANY] * 8,
        [array((2 * SEQ, 512), F32)] * 2,
        [ANY] * 2,
        scalars=scalars,
        tokens=tokens,
        scratch=[
            pltpu.VMEM((2, 4, 2 * SEQ, 1024), BF),
            pltpu.VMEM((4, 1024, 512), BF),
            pltpu.VMEM((2, 2 * SEQ, 512), F32),
            pltpu.SemaphoreType.DMA((2, 5)),
            pltpu.SemaphoreType.DMA((4, 2, 2)),
        ],
        us=16,
    )


def finish_kernel(pair, s_ref, *refs):
    errs = jnp.zeros((1, 128), F32)
    if pair == 1:
        errs = refs[1][...]
        refs = refs[2:]
    keep_ref, got_ref, target_ref, out_ref, err_ref = refs
    target = target_ref[0].astype(F32)
    lane = lax.broadcasted_iota(jnp.int32, (1, 128), 1)
    for m in range(2):
        rows = slice(m * SEQ, (m + 1) * SEQ)
        out = (keep_ref[rows, :] + got_ref[rows, :].astype(F32)).astype(BF)
        out_ref[m] = out
        gap = out.astype(F32) - target
        err = jnp.sum(gap * gap)
        errs = errs + jnp.where(lane == 4 * s_ref[0] + 2 * pair + m, err, 0.0)
    err_ref[...] = errs


def finish(scalars, pair, keep, got, targets, done=()):
    return pl.pallas_call(
        functools.partial(finish_kernel, pair),
        grid_spec=pltpu.PrefetchScalarGridSpec(
            num_scalar_prefetch=1,
            grid=(1,),
            in_specs=([ANY, whole((1, 128))] if done else [])
            + [whole((2 * SEQ, 512))] * 2
            + [pl.BlockSpec((1, SEQ, 512), lambda i, s: (pair, 0, 0))],
            out_specs=[pl.BlockSpec((2, SEQ, 512), lambda i, s: (pair, 0, 0)), whole((1, 128))],
        ),
        out_shape=[array((4, SEQ, 512), BF), array((1, 128), F32)],
        input_output_aliases={1: 0} if done else {},
        compiler_params=pltpu.CompilerParams(vmem_limit_bytes=64 * 2**20),
        cost_estimate=pl.CostEstimate(flops=2**31, bytes_accessed=2**20, transcendentals=0),
        name="finish",
    )(scalars, *done, keep, got, targets)


def outer(left, right):
    high = left.astype(BF)
    low = (left - high.astype(F32)).astype(BF)
    left = jnp.concatenate([high, low], 0)
    right = jnp.concatenate([right, right], 0)
    return lax.dot_general(left, right, (((0,), (0,)), ((), ())), preferred_element_type=F32)


def update_kernel(err_ref, lk_ref, rk_ref, lv_ref, rv_ref, key_ref, value_ref):
    err = jnp.sum(err_ref[...], axis=1) / (SEQ * D)
    lane = lax.broadcasted_iota(jnp.int32, err.shape, 1)
    used = lane < 8
    mean = jnp.sum(jnp.where(used, err, 0.0)) / 128
    var = jnp.sum(jnp.where(used, (err - mean) * (err - mean), 0.0)) / 128
    spread = jnp.sqrt(jnp.full((1, 1), var + 1e-05, F32))
    diff = err - pltpu.roll(err, 127, 1)
    coef = jnp.concatenate([diff[:, i : i + 1] for i in (0, 2, 4, 6)], 0) / (spread * math.sqrt(64))
    key_ref[...] = outer(lk_ref[...].astype(F32) * coef, rk_ref[...])
    value_ref[...] = outer(lv_ref[...].astype(F32) * coef, rv_ref[...])


def update(err, left_key, right_key, left_value, right_value):
    args = [err, left_key, right_key, left_value, right_value]
    return call(
        update_kernel,
        "update",
        args,
        [whole(v.shape) for v in args],
        [array((128, 1024), F32), array((1024, 128), F32)],
        [whole((128, 1024)), whole((1024, 128))],
    )


def per_device(
    inputs,
    mix_key,
    key_weight,
    value_weight,
    key_left,
    key_right,
    value_left,
    value_right,
    pair_sign,
    targets,
):
    pop, mp = lax.axis_index("pop"), lax.axis_index("mp")
    x, zh, c = pop // 8, (pop // 2) % 4, pop % 2
    y, zl = mp // 2, mp % 2
    i32 = lambda *v: jnp.stack([jnp.asarray(e, jnp.int32) for e in v])

    def swap(values):
        return [move(v, c=1) for v in values]

    own_x, key_z = ring(key_weight, "x"), ring(key_weight, "zh")
    moved = transpose_xy(value_weight)
    rest = join([key_z[1], key_z[3], key_z[2]], [own_x[2], own_x[3], moved])
    mine, its, probe = mix(i32(c), inputs, mix_key, key_left, [rest])
    rest = [rest, step(rest, "x"), None, step(rest, "x", -1)]
    value_z = [moved, step(moved, "zh"), None, step(moved, "zh", -1)]
    def to_owner(v):
        return v.reshape(2, 32, 128).transpose(1, 0, 2)

    def to_all(v):
        return jnp.broadcast_to(v.reshape(1, 16, 128), (32, 16, 128))

    sign = pair_sign.astype(BF)[:, None]
    parcel = jnp.concatenate(
        [
            to_owner(key_left * sign),
            to_owner(value_right),
            to_all(key_right),
            to_all(value_left * sign),
        ],
        1,
    )
    right = value_right.astype(F32)
    send_right, keep_right = (
        lax.dynamic_slice_in_dim(right, (2 * y + half) * 512, 512, 1) for half in (1 - zl, zl)
    )
    at = [i32(x, c, y, pair_sign[p]) for p in range(2)]
    rest[1], value_z[1] = fence([rest[1], value_z[1]], [rest[3], parcel, send_right, keep_right, *at], us=24)
    rest[2], value_z[2] = step(rest[1], "x"), step(value_z[1], "zh")
    me = i32(x, zh, c)
    got = move(its, c=1)
    acc, other = both_step(me, mine, got, own_x, [rest[0], rest[1], rest[3]])
    slots = [(zh + (2 * c - 1) * k) % 4 for k in range(4)]
    slots = i32(*[jnp.where(s // 2 == zl, 2, 0) + s % 2 for s in slots])
    value_x = order(slots, value_z)
    (other,) = fence([other], [value_z[2], value_z[3]])
    got = move(other, c=1)
    vecs = [key_right, value_left]
    base = last_step(me, mine, its, acc, got, *vecs, [rest[2], move(rest[2], c=1)], [value_x])

    (value_x,) = fence([value_x], [base])
    value_x = [value_x, step(value_x, "x"), None, step(value_x, "x", -1)]
    value_w = [move(value_x[0], c=1)]
    near = [base, step(base, "y"), None, step(base, "y", -1)]

    (parcel,) = fence([parcel], [base])
    parcel = lax.all_to_all(parcel, "pop", split_axis=0, concat_axis=0, tiled=True)

    def unpack(lo, hi):
        v = parcel[:, lo:hi].reshape(16, 2, 2, (hi - lo) // 2 * 128)
        return v.transpose(1, 2, 0, 3).reshape(64, (hi - lo) // 2 * 128)

    left_key, right_value = unpack(0, 2), unpack(2, 4)
    right_key, left_value = unpack(4, 20), unpack(20, 36)
    value_x[1], near[1] = fence(
        [value_x[1], near[1]], [value_x[3], near[3], parcel]
    )
    value_x[2], near[2] = step(value_x[1], "x"), step(near[1], "y")
    value_w = (value_x, value_w + swap(value_x[1:]))

    hidden, got = [], []
    for p in range(2):
        send, *hid = send_step(at[p], near, probe, p, send_right, *value_w)
        hidden.append((send, *hid))
        got.append(move(send, zl=1))
    sends, hids, sides = zip(*hidden)
    keep = keep_step(at[0], hids, sides, keep_right, *value_w, sends)
    done = finish(i32(c), 0, keep[0], got[0], targets)
    outputs, err = finish(i32(c), 1, keep[1], got[1], targets, done)

    err = err + move(err, c=1)
    err = jnp.broadcast_to(err[None], (128, 1, 128))
    groups = [[place(at["x"], at["zh"], core, at["y"], at["zl"]) for at in everywhere() if at["c"] == core] for core in range(2)]
    err = lax.all_to_all(
        err, AXES, split_axis=0, concat_axis=0, tiled=True, axis_index_groups=groups
    )
    key_update, value_update = update(
        err.reshape(16, 8, 128), left_key, right_key, left_value, right_value
    )
    return outputs, key_update, value_update


def solution(mesh):
    in_specs = (
        P("pop", None, None),
        P(),
        P("pop", "mp"),
        P("mp", "pop"),
        P("pop", None),
        P("pop", "mp"),
        P("pop", "mp"),
        P("pop", None),
        P("pop"),
        P("pop", None, "mp"),
    )
    out_specs = (P("pop", None, "mp"), P("pop", "mp"), P("mp", "pop"))
    return jax.shard_map(
        per_device, mesh=mesh, in_specs=in_specs, out_specs=out_specs, check_vma=False
    )
```
